32 devices in a mesh: grp: 2 (over x), ctx: 16 (over z, y, core).
Axes of the slice: x: 2, y: 2, z: 4, core: 2. Of those that a mesh axis runs over, the one named last changes fastest.
Arguments:
- query_series: bfloat16 [4096, 2048], P(('grp', 'ctx')), parts along dimension 0, may hold values from -6 to 6
- key_series: bfloat16 [4096, 2048], P(('grp', 'ctx')), parts along dimension 0, may hold values from -6 to 6
- value_series: bfloat16 [4096, 2048], P(('grp', 'ctx')), parts along dimension 0, may hold values from -6 to 6
- grad_out: bfloat16 [4096, 2048], P(('grp', 'ctx')), parts along dimension 0, may hold values from -6 to 6
- gate_mask: int32 [4096], P(('grp', 'ctx')), parts along dimension 0, may hold values 0 or 1
- filter_spectrum: float32 [2, 32, 128, 2048], P(None, 'ctx'), may hold values from -6 to 6
Outputs:
- mixer_out: bfloat16 [4096, 2048], P(('grp', 'ctx')), parts along dimension 0
- grad_queries: bfloat16 [4096, 2048], P(('grp', 'ctx')), parts along dimension 0
- grad_keys: bfloat16 [4096, 2048], P(('grp', 'ctx')), parts along dimension 0
- grad_values: bfloat16 [4096, 2048], P(('grp', 'ctx')), parts along dimension 0
- grad_spectrum: float32 [2, 64, 128, 2048], P(None, ('grp', 'ctx')), parts along dimension 1
The draws below stay inside these ranges and needn't reach their ends.
There are 2 independent parts, one for each index of `grp`. The reference program is written for one: setup_inputs(seed, part) draws one part's arguments, and reference() takes and returns one part's arrays. A program takes and returns all parts, laid end to end along the dimension named above; an argument that names none is the same for every part. Nothing has to cross between parts.
All inputs are finite; a program needn't handle non-finite values. No bound on the sum of `gate_mask` on one device may be relied on, other than what follows from the above.
Results may differ from the reference program's by a relative error of at most 0.0051.
Values may be sent and summed in bfloat16 or wider, within the bound.
A program may use at most 128 MiB of HBM per device.

```python
import jax
import jax.numpy as jnp
import numpy as np
from jax import lax

CH = 2048
TOK_DEV = 128
SEQ = 2048
CLASSES = 32
N_CTX = 16


def with_ends(values, stream_key, smallest, largest):
    shape = values.shape
    index_at = [jax.random.randint(jax.random.fold_in(stream_key, axis), (), 0, shape[axis]) for axis in range(len(shape))]
    values = values.at[tuple(index_at)].set(smallest)
    longest = shape.index(max(shape))
    index_at[longest] = (index_at[longest] + 1) % shape[longest]
    return values.at[tuple(index_at)].set(largest)


def block_scale(own_key, extent, shards, low, largest):
    def one(axis_at, blocks):
        heights = jax.random.uniform(jax.random.fold_in(jax.random.fold_in(own_key, 6), axis_at), (blocks,), jnp.float32, low / len(shards), largest / len(shards))
        return jnp.repeat(jnp.exp(heights), extent[axis_at] // blocks).reshape((-1,) + (1,) * (len(extent) - axis_at - 1))

    factor_of = one(*shards[0])
    for cut in shards[1:]:
        factor_of = factor_of * one(*cut)
    return factor_of


def normal_values(own_key, shape, scale, reach, split=(), dtype=jnp.bfloat16):
    level = block_scale(own_key, shape, split, -0.22, 0.18) if split else 1.0
    values = jax.random.normal(own_key, shape, jnp.float32) * scale * level
    return jnp.minimum(jnp.maximum(values, -reach), reach).astype(dtype)


def setup_inputs(seed: int = 0, part: int = 0) -> dict:
    key_list = jax.random.split(jax.random.key(seed), 7)
    part_splits = jax.random.split(jax.random.fold_in(key_list[6], part), 7)
    return {
        "query_series": normal_values(part_splits[0], (SEQ, CH), 1.0, 6.0, ((0, 16),)),
        "key_series": normal_values(part_splits[1], (SEQ, CH), 1.0, 6.0, ((0, 16),)),
        "value_series": normal_values(part_splits[2], (SEQ, CH), 1.0, 6.0, ((0, 16),)),
        "grad_out": normal_values(part_splits[3], (SEQ, CH), 1.0, 6.0, ((0, 16),)),
        "gate_mask": with_ends((jax.random.randint(part_splits[4], (SEQ,), 0, 4) < 3).astype(jnp.int32), jax.random.fold_in(part_splits[4], 1), 0, 1),
        "filter_spectrum": normal_values(key_list[5], (2, CLASSES, TOK_DEV, CH), 1.0, 6.0, ((1, 16),), jnp.float32),
    }


def class_order(devices):
    indices = np.arange(2 * devices)
    pair_index = indices // 2
    parity = indices % 2
    return np.where(pair_index == 0, parity * devices, np.where(parity == 0, pair_index, 2 * devices - pair_index))


def reference(query_series, key_series, value_series, grad_out, gate_mask, filter_spectrum):
    ordering = class_order(N_CTX)
    undo_order = np.argsort(ordering)
    gating = gate_mask.astype(jnp.float32)[:, None]
    gated_pair = (gating * key_series.astype(jnp.float32) * value_series.astype(jnp.float32)).astype(jnp.bfloat16)
    back_signal = (query_series.astype(jnp.float32) * grad_out.astype(jnp.float32)).astype(jnp.bfloat16)
    span_width = min(CH, 256)
    groups_count = CH // span_width

    def to_blocks(array):
        return jnp.moveaxis(array.reshape(array.shape[:-1] + (groups_count, span_width)), -2, 0)

    def from_blocks(array):
        moved = jnp.moveaxis(array, 0, -2)
        return moved.reshape(moved.shape[:-2] + (CH,))

    def forward(series):
        widened = series.astype(jnp.float32)
        padded = jnp.concatenate([widened, jnp.zeros_like(widened)], axis=0)
        spectrum = jnp.fft.fft(padded, axis=0, norm="ortho")
        spectrum = spectrum.reshape(TOK_DEV, CLASSES, span_width).transpose(1, 0, 2)
        return spectrum[ordering]

    def backward(spectrum):
        natural = spectrum[undo_order].transpose(1, 0, 2).reshape(2 * SEQ, span_width)
        return jnp.real(jnp.fft.ifft(natural, axis=0, norm="ortho"))[:SEQ]

    def channel_block(operands):
        gated_block, back_block, spec_block = operands
        signal = forward(gated_block)
        adjoint = forward(back_block)
        response = spec_block[0] + 1j * spec_block[1]
        conv_out = backward(signal * response)
        grad_mixed = backward(adjoint * jnp.conj(response))
        grad_real = jnp.real(jnp.conj(adjoint) * signal)
        grad_imag = jnp.imag(adjoint * jnp.conj(signal))
        return conv_out, grad_mixed, jnp.stack([grad_real, grad_imag])

    conv_blocks, mixed_blocks, spec_blocks = lax.map(channel_block, (to_blocks(gated_pair), to_blocks(back_signal), to_blocks(filter_spectrum)))
    conv = from_blocks(conv_blocks)
    grad_mixed = from_blocks(mixed_blocks)
    grad_spectrum = from_blocks(spec_blocks)
    mixer_out = (query_series.astype(jnp.float32) * conv).astype(jnp.bfloat16)
    grad_queries = (grad_out.astype(jnp.float32) * conv).astype(jnp.bfloat16)
    grad_keys = (grad_mixed * gating * value_series.astype(jnp.float32)).astype(jnp.bfloat16)
    grad_values = (grad_mixed * gating * key_series.astype(jnp.float32)).astype(jnp.bfloat16)
    return mixer_out, grad_queries, grad_keys, grad_values, grad_spectrum
```

```python
import functools
import math

import jax
import jax.numpy as jnp
import numpy as np
from jax import lax
from jax.experimental import pallas as pl
from jax.experimental.pallas import tpu as pltpu
from jax.sharding import PartitionSpec as P

highest = lax.Precision.HIGHEST


def class_order(devices):
    indices = np.arange(2 * devices)
    pair_index = indices // 2
    parity = indices % 2
    return np.where(
        pair_index == 0,
        parity * devices,
        np.where(parity == 0, pair_index, 2 * devices - pair_index),
    )


def partner(spectrum):
    flipped = jnp.flip(spectrum, axis=-2)
    crossed = jnp.flip(flipped, axis=-3)
    anchor_head = jnp.roll(flipped[..., 0:1, :, :], 1, axis=-2)
    anchor = jnp.concatenate([anchor_head, flipped[..., 1:2, :, :]], axis=-3)
    return jnp.where(lax.axis_index("ctx") == 0, anchor, crossed)


def forward_spectra(series):
    devices = lax.axis_size("ctx")
    tok_rows = series.shape[1]
    group_rows = tok_rows // devices
    classes = 2 * devices
    fft_length = classes * tok_rows
    ordering = class_order(devices)
    norm_factor = 1.0 / math.sqrt(fft_length)
    positions = lax.axis_index("ctx") * group_rows + jnp.arange(group_rows, dtype=jnp.int32)
    offsets = jnp.arange(devices, dtype=jnp.int32) * tok_rows
    order_column = jnp.asarray(ordering, jnp.int32)[:, None, None]
    first_turns = order_column * (offsets[None, :, None] + positions[None, None, :]) % fft_length
    first_angle = first_turns.astype(jnp.float32) * (-2.0 * math.pi / fft_length)
    first_table = jnp.stack([jnp.cos(first_angle), jnp.sin(first_angle)])
    rows_index = np.arange(tok_rows)
    second_angle = 2.0 * np.pi * (np.outer(rows_index, rows_index) % tok_rows) / tok_rows
    cos_second = np.cos(second_angle)
    sin_second = -np.sin(second_angle)
    row_real = np.stack([cos_second, -sin_second], axis=1)
    row_imag = np.stack([sin_second, cos_second], axis=1)
    second_table = jnp.asarray(np.stack([row_real, row_imag]) * norm_factor, jnp.float32)
    shaped = series.reshape(2, devices, group_rows, series.shape[-1])
    received = lax.all_to_all(shaped, "ctx", split_axis=1, concat_axis=1, tiled=True)
    channels = received.shape[-1]
    widened = received.astype(jnp.float32)
    parts = jnp.einsum("qjab,sabx->sqjbx", first_table, widened, precision=highest)
    parts = jnp.stack([parts[0, 0] - parts[1, 1], parts[0, 1] + parts[1, 0]])[None]
    signals = parts.shape[0]
    stacked = parts.reshape(signals * 2, devices, 2, group_rows, channels)
    received = lax.all_to_all(stacked, "ctx", split_axis=1, concat_axis=3, tiled=True)
    channels = received.shape[-1]
    signals = received.shape[0] // 2
    shaped = received.reshape(signals, 2, 2, tok_rows, channels)
    joined = jnp.einsum("qdpb,speby->sqedy", second_table, shaped, precision=highest)
    spectrum = joined.reshape(signals * 2, 2, tok_rows, channels)
    return spectrum.reshape(spectrum.shape[0] // 2, 2, 2, tok_rows, series.shape[-1])


def inverse_series(spectra):
    devices = lax.axis_size("ctx")
    signals = spectra.shape[0]
    tok_rows = spectra.shape[3]
    channels_all = spectra.shape[4]
    group_rows = tok_rows // devices
    classes = 2 * devices
    fft_length = classes * tok_rows
    ordering = class_order(devices)
    norm_factor = 1.0 / math.sqrt(fft_length)
    location = lax.axis_index("ctx")
    own_classes = jnp.stack(
        [
            jnp.where(location == 0, 0, location),
            jnp.where(location == 0, devices, classes - location),
        ]
    )
    rows_index = jnp.arange(tok_rows, dtype=jnp.int32)
    square_turns = rows_index[:, None] * rows_index[None, :] * classes % fft_length
    second_turns = (
        square_turns[None, :, :] + own_classes[:, None, None] * rows_index[None, :, None]
    ) % fft_length
    second_angle = second_turns.astype(jnp.float32) * (2.0 * math.pi / fft_length)
    cos_second = jnp.cos(second_angle)
    sin_second = jnp.sin(second_angle)
    second_table = jnp.stack(
        [jnp.stack([cos_second, -sin_second], axis=2), jnp.stack([sin_second, cos_second], axis=2)],
        axis=1,
    )
    stacked = jnp.einsum("eqbpd,spedy->sqeby", second_table, spectra, precision=highest)
    stacked = stacked.reshape(signals * 2, 1, 2, tok_rows, channels_all)
    first_angle = 2.0 * np.pi * (np.outer(np.arange(devices), ordering) % classes) / classes
    cos_first = np.cos(first_angle)
    sin_first = np.sin(first_angle)
    full_table = (
        np.stack(
            [np.stack([cos_first, -sin_first], axis=1), np.stack([sin_first, cos_first], axis=1)]
        )
        * norm_factor
    )
    first_table = jnp.asarray(full_table, jnp.float32)
    received = lax.all_to_all(stacked, "ctx", split_axis=3, concat_axis=1, tiled=True)
    channels = received.shape[-1]
    flattened = received.reshape(signals, 2, classes, group_rows * channels)
    time_series = jnp.einsum("qapj,spjx->sqax", first_table, flattened, precision=highest)
    time_series = time_series.reshape(2, devices, group_rows, channels)
    outputs = lax.all_to_all(time_series, "ctx", split_axis=1, concat_axis=1, tiled=True)
    return outputs.reshape(2, tok_rows, channels_all)


def narrow_shards(query_series, key_series, value_series, grad_out, gate_mask, filter_spectrum):
    gating = gate_mask.astype(jnp.float32)[:, None]
    gated_pair = (
        gating * key_series.astype(jnp.float32) * value_series.astype(jnp.float32)
    ).astype(jnp.bfloat16)
    back_signal = (query_series.astype(jnp.float32) * grad_out.astype(jnp.float32)).astype(
        jnp.bfloat16
    )
    series = jnp.stack([gated_pair, back_signal])
    filter_real = filter_spectrum[0]
    filter_imag = filter_spectrum[1]
    combined = forward_spectra(series)[0]
    mirror = partner(combined)
    signal_real = 0.5 * (combined[0] + mirror[0])
    signal_imag = 0.5 * (combined[1] - mirror[1])
    adjoint_real = 0.5 * (combined[1] + mirror[1])
    adjoint_imag = 0.5 * (mirror[0] - combined[0])
    conv_real = signal_real * filter_real - signal_imag * filter_imag
    conv_imag = signal_real * filter_imag + signal_imag * filter_real
    back_real = adjoint_real * filter_real + adjoint_imag * filter_imag
    back_imag = adjoint_imag * filter_real - adjoint_real * filter_imag
    grad_spectrum = jnp.stack(
        [
            adjoint_real * signal_real + adjoint_imag * signal_imag,
            adjoint_imag * signal_real - adjoint_real * signal_imag,
        ]
    )
    minus_pair = jnp.stack([conv_real + back_imag, conv_imag - back_real])
    mirror_back = partner(minus_pair)
    joined = jnp.stack(
        [
            0.5 * (conv_real - back_imag + mirror_back[0]),
            0.5 * (conv_imag + back_real - mirror_back[1]),
        ]
    )
    outputs = inverse_series(joined[None])
    conv_out = outputs[0]
    grad_mixed = outputs[1]
    mixer_out = (query_series.astype(jnp.float32) * conv_out).astype(jnp.bfloat16)
    grad_queries = (grad_out.astype(jnp.float32) * conv_out).astype(jnp.bfloat16)
    grad_keys = (grad_mixed * gating * value_series.astype(jnp.float32)).astype(jnp.bfloat16)
    grad_values = (grad_mixed * gating * key_series.astype(jnp.float32)).astype(jnp.bfloat16)
    return (mixer_out, grad_queries, grad_keys, grad_values, grad_spectrum)


SUB = 16
LANES = 128


def split_table(values):
    exact = np.asarray(values, np.float32)
    high = exact.astype(jnp.bfloat16)
    low = (exact - high.astype(np.float32)).astype(jnp.bfloat16)
    return np.stack([high, low], axis=-3)


def device_tables(devices):
    classes = 2 * devices
    turns = 2.0 * np.pi * (np.outer(np.arange(devices), np.arange(devices)) % classes) / classes
    small = np.stack([np.cos(turns), -np.sin(turns)], axis=1)
    small[0, 1] = np.where(np.arange(devices) % 2 == 0, 1.0, -1.0)
    small = small.reshape(classes, devices)
    full = np.kron(small, np.eye(SUB))
    return split_table(full), split_table(full.T)


def row_tables(devices, rows):
    classes = 2 * devices
    length = classes * rows
    half = rows // 2
    place = np.arange(rows)
    tables = np.zeros((devices, 2, rows, 2, rows))
    for group in range(1, devices):
        freq = group + classes * place
        angle = 2.0 * np.pi * (np.outer(freq, place) % length) / length
        tables[group, 0, :, 0] = np.cos(angle)
        tables[group, 0, :, 1] = np.sin(angle)
        tables[group, 1, :, 0] = -np.sin(angle)
        tables[group, 1, :, 1] = np.cos(angle)
    for part, first in ((0, 0), (1, devices)):
        freq = first + classes * np.arange(half)
        angle = 2.0 * np.pi * (np.outer(freq, place) % length) / length
        tables[0, 0, part * half : (part + 1) * half, part] = np.cos(angle)
        tables[0, 1, part * half : (part + 1) * half, part] = -np.sin(angle)
    tables[0, 1, 0, 0] = np.where(place % 2 == 0, 1.0, -1.0)
    tables = tables.reshape(devices, 2 * rows, 2 * rows) / math.sqrt(length)
    return split_table(tables), split_table(tables.transpose(0, 2, 1))


def fold_tables(rows):
    half = rows // 2
    fold = np.zeros((2, 2, rows, 2, 2, rows))
    spread = np.zeros((2, 2, 2, rows, 2, rows))
    for d in range(rows):
        for part, sign in ((0, 1.0), (1, -1.0)):
            fold[1, part, d, part, 0, d] = 1.0
            fold[1, part, d, part, 1, rows - 1 - d] = sign
            spread[1, part, 0, d, part, d] = 1.0
            spread[1, part, 1, rows - 1 - d, part, d] = sign
    for d in range(half):
        for part, sign in ((0, 1.0), (1, -1.0)):
            if d > 0:
                fold[0, part, d, part, 0, d] = 1.0
                fold[0, part, d, part, 0, rows - d] = sign
                spread[0, part, 0, d, part, d] = 1.0
                spread[0, part, 0, rows - d, part, d] = sign
            fold[0, part, half + d, part, 1, d] = 1.0
            fold[0, part, half + d, part, 1, rows - 1 - d] = sign
            spread[0, part, 1, d, part, half + d] = 1.0
            spread[0, part, 1, rows - 1 - d, part, half + d] = sign
    fold[0, 0, 0, 0, 0, 0] = 1.0
    fold[0, 1, 0, 0, 0, half] = 1.0
    spread[0, 0, 0, 0, 0, 0] = 1.0
    spread[0, 0, 0, half, 1, 0] = 1.0
    return (
        fold.reshape(2, 2 * rows, 4 * rows).astype(jnp.bfloat16),
        spread.reshape(2, 4 * rows, 2 * rows).astype(jnp.bfloat16),
    )


def dot(left, right):
    return jnp.dot(left, right, preferred_element_type=jnp.float32)


def exchange_kernel(
    devices,
    rows,
    width,
    query_ref,
    key_ref,
    value_ref,
    grad_ref,
    gate_ref,
    filter_ref,
    fold_ref,
    mix_ref,
    unmix_ref,
    table_ref,
    back_ref,
    got_grad,
    got_series,
    send_signal,
    got_signal,
    send_filter,
    got_filter,
    mixed,
    turned,
    send_grad,
    send_series,
    send_sems,
    recv_sems,
    local_sems,
):
    me = lax.axis_index("ctx")
    barrier = pltpu.get_barrier_semaphore()

    def greet(step, _):
        pl.semaphore_signal(
            barrier,
            inc=1,
            device_id={"ctx": lax.rem(me + step, devices)},
            device_id_type=pl.DeviceIdType.MESH,
        )
        return 0

    lax.fori_loop(1, devices, greet, 0)

    def remote(kind, source, target, step_from, to):
        return pltpu.make_async_remote_copy(
            src_ref=source.at[to],
            dst_ref=target.at[step_from],
            send_sem=send_sems.at[kind, to],
            recv_sem=recv_sems.at[kind, step_from],
            device_id={"ctx": to},
            device_id_type=pl.DeviceIdType.MESH,
        )

    def start_all(kind, source, target):
        def body(step, _):
            remote(kind, source, target, me, lax.rem(me + step, devices)).start()
            return 0

        lax.fori_loop(1, devices, body, 0)

    def wait_received(kind, source, target, first=1):
        def body(step, _):
            other = lax.rem(me + devices - step, devices)
            remote(kind, source, target, other, other).wait_recv()
            return 0

        lax.fori_loop(first, devices, body, 0)

    def wait_sent(kind, source, target):
        def body(step, _):
            remote(kind, source, target, me, lax.rem(me + step, devices)).wait_send()
            return 0

        lax.fori_loop(1, devices, body, 0)

    gating = gate_ref[...]
    for to in range(devices):
        span = slice(to * width, (to + 1) * width)
        gated = gating * key_ref[:, span].astype(jnp.float32) * value_ref[:, span].astype(jnp.float32)
        back = query_ref[:, span].astype(jnp.float32) * grad_ref[:, span].astype(jnp.float32)
        send_signal[to, 0] = gated.astype(jnp.bfloat16)
        send_signal[to, 1] = back.astype(jnp.bfloat16)
    pl.semaphore_wait(barrier, devices - 1)
    start_all(0, send_signal, got_signal)
    got_signal[me] = send_signal[me]

    for to in range(devices):
        span = slice(to * width, (to + 1) * width)
        block = filter_ref[:, span]
        high = block.astype(jnp.bfloat16)
        low = (block - high.astype(jnp.float32)).astype(jnp.bfloat16)
        folded = dot(fold_ref[...], high) + dot(fold_ref[...], low)
        send_filter[to] = folded.astype(jnp.bfloat16)
    start_all(1, send_filter, got_filter)
    got_filter[me] = send_filter[me]

    wait_received(0, send_signal, got_signal)

    def mix(part, _):
        span = pl.ds(pl.multiple_of(part * SUB, SUB), SUB)
        columns = jnp.concatenate(
            [got_signal[:, which, span, :].reshape(devices * SUB, width) for which in (0, 1)], axis=1
        )
        result = dot(mix_ref[0], columns) + dot(mix_ref[1], columns)
        mixed[:, span, :] = result.astype(jnp.bfloat16).reshape(2 * devices, SUB, 2 * width)
        return 0

    lax.fori_loop(0, rows // SUB, mix, 0)
    wait_received(1, send_filter, got_filter)

    row_index = lax.broadcasted_iota(jnp.int32, (rows, width), 0)

    def one_group(group, _):
        source = mixed[pl.ds(2 * group, 2)].reshape(2 * rows, 2 * width)
        spectra = dot(table_ref[group, 0], source) + dot(table_ref[group, 1], source)
        signal_real = spectra[:rows, :width]
        signal_imag = spectra[rows:, :width]
        adjoint_real = spectra[:rows, width:]
        adjoint_imag = spectra[rows:, width:]
        response = got_filter[group].astype(jnp.float32)
        filter_real = response[:rows]
        filter_imag = response[rows:]
        real_pair = jnp.logical_and(row_index == 0, group == 0)

        def times(first_real, first_imag, second_real, second_imag, sign):
            both = first_imag * second_imag
            real = first_real * second_real - jnp.where(real_pair, 0.0, sign * both)
            imag = jnp.where(real_pair, both, first_imag * second_real + sign * first_real * second_imag)
            return real, imag

        grad_real, grad_imag = times(adjoint_real, adjoint_imag, signal_real, signal_imag, -1.0)
        send_grad[group, :rows] = grad_real.astype(jnp.bfloat16)
        send_grad[group, rows:] = grad_imag.astype(jnp.bfloat16)

        @pl.when(group != me)
        def _():
            remote(2, send_grad, got_grad, me, group).start()

        conv_real, conv_imag = times(signal_real, signal_imag, filter_real, filter_imag, 1.0)
        back_real, back_imag = times(adjoint_real, adjoint_imag, filter_real, filter_imag, -1.0)
        product = jnp.concatenate(
            [
                jnp.concatenate([conv_real, back_real], axis=1),
                jnp.concatenate([conv_imag, back_imag], axis=1),
            ],
            axis=0,
        ).astype(jnp.bfloat16)
        result = dot(back_ref[group, 0], product) + dot(back_ref[group, 1], product)
        turned[pl.ds(2 * group, 2)] = result.astype(jnp.bfloat16).reshape(2, rows, 2 * width)
        return 0

    lax.fori_loop(0, devices, one_group, 0)
    own_grad = pltpu.make_async_copy(send_grad.at[me], got_grad.at[me], local_sems.at[0])
    own_grad.start()

    def unmix(part, _):
        span = pl.ds(pl.multiple_of(part * SUB, SUB), SUB)
        columns = turned[:, span, :].reshape(2 * devices * SUB, 2 * width)
        result = dot(unmix_ref[0], columns) + dot(unmix_ref[1], columns)
        result = result.astype(jnp.bfloat16).reshape(devices, SUB, 2 * width)
        send_series[:, 0, span, :] = result[:, :, :width]
        send_series[:, 1, span, :] = result[:, :, width:]
        return 0

    lax.fori_loop(0, rows // SUB, unmix, 0)
    start_all(3, send_series, got_series)
    own_series = pltpu.make_async_copy(send_series.at[me], got_series.at[me], local_sems.at[1])
    own_series.start()
    own_grad.wait()
    own_series.wait()
    wait_received(2, send_grad, got_grad)
    wait_received(3, send_series, got_series)
    for kind, source, target in (
        (0, send_signal, got_signal),
        (1, send_filter, got_filter),
        (2, send_grad, got_grad),
        (3, send_series, got_series),
    ):
        wait_sent(kind, source, target)


def finish_kernel(
    blocks,
    width,
    query_ref,
    key_ref,
    value_ref,
    grad_ref,
    gate_ref,
    spread_ref,
    half_ref,
    series_ref,
    mixer_out,
    queries_out,
    keys_out,
    values_out,
    spectrum_out,
):
    gating = gate_ref[...]
    for block in range(blocks):
        span = slice(block * width, (block + 1) * width)
        conv = series_ref[block, 0].astype(jnp.float32)
        back = series_ref[block, 1].astype(jnp.float32) * gating
        mixer_out[:, span] = (query_ref[:, span].astype(jnp.float32) * conv).astype(jnp.bfloat16)
        queries_out[:, span] = (grad_ref[:, span].astype(jnp.float32) * conv).astype(jnp.bfloat16)
        keys_out[:, span] = (back * value_ref[:, span].astype(jnp.float32)).astype(jnp.bfloat16)
        values_out[:, span] = (back * key_ref[:, span].astype(jnp.float32)).astype(jnp.bfloat16)
        spectrum_out[:, span] = dot(spread_ref[...], half_ref[block])


def wide_shards(query_series, key_series, value_series, grad_out, gate_mask, filter_spectrum):
    devices = lax.axis_size("ctx")
    rows, channels = query_series.shape
    width = channels // devices
    gating = gate_mask.astype(jnp.float32)[:, None]
    mix_table, unmix_table = device_tables(devices)
    forward_table, back_table = row_tables(devices, rows)
    folds, spreads = fold_tables(rows)
    first = lax.axis_index("ctx") == 0
    fold = jnp.where(first, folds[0], folds[1])
    spread = jnp.where(first, spreads[0], spreads[1])
    half = jnp.bfloat16
    vmem = pl.BlockSpec(memory_space=pltpu.VMEM)
    anywhere = pl.BlockSpec(memory_space=pl.ANY)
    spectrum_block = (devices, 2 * rows, width)
    series_block = (devices, 2, rows, width)
    got_grad, got_series = pl.pallas_call(
        functools.partial(exchange_kernel, devices, rows, width),
        out_shape=(
            jax.ShapeDtypeStruct(spectrum_block, half),
            jax.ShapeDtypeStruct(series_block, half),
        ),
        in_specs=[vmem] * 11,
        out_specs=(anywhere, anywhere),
        scratch_shapes=[
            pltpu.VMEM(series_block, half),
            pltpu.VMEM(series_block, half),
            pltpu.VMEM(spectrum_block, half),
            pltpu.VMEM(spectrum_block, half),
            pltpu.VMEM((2 * devices, rows, 2 * width), half),
            pltpu.VMEM((2 * devices, rows, 2 * width), half),
            pltpu.VMEM(spectrum_block, half),
            pltpu.VMEM(series_block, half),
            pltpu.SemaphoreType.DMA((4, devices)),
            pltpu.SemaphoreType.DMA((4, devices)),
            pltpu.SemaphoreType.DMA((2,)),
        ],
        compiler_params=pltpu.CompilerParams(
            collective_id=0, has_side_effects=True, vmem_limit_bytes=48 * 1024 * 1024
        ),
        name="exchange",
    )(
        query_series,
        key_series,
        value_series,
        grad_out,
        gating,
        filter_spectrum.reshape(4 * rows, channels),
        fold,
        jnp.asarray(mix_table),
        jnp.asarray(unmix_table),
        jnp.asarray(forward_table),
        jnp.asarray(back_table),
    )
    blocks = 2
    columns = pl.BlockSpec((rows, blocks * width), lambda step: (0, step))
    mixer_out, queries, keys, values, spectrum = pl.pallas_call(
        functools.partial(finish_kernel, blocks, width),
        grid=(devices // blocks,),
        out_shape=(jax.ShapeDtypeStruct((rows, channels), half),) * 4
        + (jax.ShapeDtypeStruct((4 * rows, channels), jnp.float32),),
        in_specs=[
            columns,
            columns,
            columns,
            columns,
            pl.BlockSpec((rows, 1), lambda step: (0, 0)),
            pl.BlockSpec((4 * rows, 2 * rows), lambda step: (0, 0)),
            pl.BlockSpec((blocks, 2 * rows, width), lambda step: (step, 0, 0)),
            pl.BlockSpec((blocks, 2, rows, width), lambda step: (step, 0, 0, 0)),
        ],
        out_specs=(columns,) * 4 + (pl.BlockSpec((4 * rows, blocks * width), lambda step: (0, step)),),
        compiler_params=pltpu.CompilerParams(vmem_limit_bytes=32 * 1024 * 1024),
        name="finish",
    )(query_series, key_series, value_series, grad_out, gating, spread, got_grad, got_series)
    return mixer_out, queries, keys, values, spectrum.reshape(2, 2, rows, channels)


def shards(query_series, *others):
    devices = lax.axis_size("ctx")
    rows, channels = query_series.shape
    if rows % SUB == 0 and channels % (devices * LANES) == 0:
        return wide_shards(query_series, *others)
    return narrow_shards(query_series, *others)


def solution(mesh):
    placed = (
        P(("grp", "ctx"), None),
        P(("grp", "ctx"), None),
        P(("grp", "ctx"), None),
        P(("grp", "ctx"), None),
        P(("grp", "ctx")),
        P(None, "ctx", None, None),
    )
    return jax.shard_map(
        shards,
        mesh=mesh,
        in_specs=placed,
        out_specs=(
            P(("grp", "ctx"), None),
            P(("grp", "ctx"), None),
            P(("grp", "ctx"), None),
            P(("grp", "ctx"), None),
            P(None, ("grp", "ctx"), None, None),
        ),
        check_vma=False,
    )
```

```python
import functools
import math

import jax
import jax.numpy as jnp
import numpy as np
from jax import lax
from jax.experimental import pallas as pl
from jax.experimental.pallas import tpu as pltpu
from jax.sharding import PartitionSpec as P

highest = lax.Precision.HIGHEST


def class_order(devices):
    indices = np.arange(2 * devices)
    pair_index = indices // 2
    parity = indices % 2
    return np.where(
        pair_index == 0,
        parity * devices,
        np.where(parity == 0, pair_index, 2 * devices - pair_index),
    )


def partner(spectrum):
    flipped = jnp.flip(spectrum, axis=-2)
    crossed = jnp.flip(flipped, axis=-3)
    anchor_head = jnp.roll(flipped[..., 0:1, :, :], 1, axis=-2)
    anchor = jnp.concatenate([anchor_head, flipped[..., 1:2, :, :]], axis=-3)
    return jnp.where(lax.axis_index("ctx") == 0, anchor, crossed)


def forward_spectra(series):
    devices = lax.axis_size("ctx")
    tok_rows = series.shape[1]
    group_rows = tok_rows // devices
    classes = 2 * devices
    fft_length = classes * tok_rows
    ordering = class_order(devices)
    norm_factor = 1.0 / math.sqrt(fft_length)
    positions = lax.axis_index("ctx") * group_rows + jnp.arange(group_rows, dtype=jnp.int32)
    offsets = jnp.arange(devices, dtype=jnp.int32) * tok_rows
    order_column = jnp.asarray(ordering, jnp.int32)[:, None, None]
    first_turns = order_column * (offsets[None, :, None] + positions[None, None, :]) % fft_length
    first_angle = first_turns.astype(jnp.float32) * (-2.0 * math.pi / fft_length)
    first_table = jnp.stack([jnp.cos(first_angle), jnp.sin(first_angle)])
    rows_index = np.arange(tok_rows)
    second_angle = 2.0 * np.pi * (np.outer(rows_index, rows_index) % tok_rows) / tok_rows
    cos_second = np.cos(second_angle)
    sin_second = -np.sin(second_angle)
    row_real = np.stack([cos_second, -sin_second], axis=1)
    row_imag = np.stack([sin_second, cos_second], axis=1)
    second_table = jnp.asarray(np.stack([row_real, row_imag]) * norm_factor, jnp.float32)
    shaped = series.reshape(2, devices, group_rows, series.shape[-1])
    received = lax.all_to_all(shaped, "ctx", split_axis=1, concat_axis=1, tiled=True)
    channels = received.shape[-1]
    widened = received.astype(jnp.float32)
    parts = jnp.einsum("qjab,sabx->sqjbx", first_table, widened, precision=highest)
    parts = jnp.stack([parts[0, 0] - parts[1, 1], parts[0, 1] + parts[1, 0]])[None]
    signals = parts.shape[0]
    stacked = parts.reshape(signals * 2, devices, 2, group_rows, channels)
    received = lax.all_to_all(stacked, "ctx", split_axis=1, concat_axis=3, tiled=True)
    channels = received.shape[-1]
    signals = received.shape[0] // 2
    shaped = received.reshape(signals, 2, 2, tok_rows, channels)
    joined = jnp.einsum("qdpb,speby->sqedy", second_table, shaped, precision=highest)
    spectrum = joined.reshape(signals * 2, 2, tok_rows, channels)
    return spectrum.reshape(spectrum.shape[0] // 2, 2, 2, tok_rows, series.shape[-1])


def inverse_series(spectra):
    devices = lax.axis_size("ctx")
    signals = spectra.shape[0]
    tok_rows = spectra.shape[3]
    channels_all = spectra.shape[4]
    group_rows = tok_rows // devices
    classes = 2 * devices
    fft_length = classes * tok_rows
    ordering = class_order(devices)
    norm_factor = 1.0 / math.sqrt(fft_length)
    location = lax.axis_index("ctx")
    own_classes = jnp.stack(
        [
            jnp.where(location == 0, 0, location),
            jnp.where(location == 0, devices, classes - location),
        ]
    )
    rows_index = jnp.arange(tok_rows, dtype=jnp.int32)
    square_turns = rows_index[:, None] * rows_index[None, :] * classes % fft_length
    second_turns = (
        square_turns[None, :, :] + own_classes[:, None, None] * rows_index[None, :, None]
    ) % fft_length
    second_angle = second_turns.astype(jnp.float32) * (2.0 * math.pi / fft_length)
    cos_second = jnp.cos(second_angle)
    sin_second = jnp.sin(second_angle)
    second_table = jnp.stack(
        [jnp.stack([cos_second, -sin_second], axis=2), jnp.stack([sin_second, cos_second], axis=2)],
        axis=1,
    )
    stacked = jnp.einsum("eqbpd,spedy->sqeby", second_table, spectra, precision=highest)
    stacked = stacked.reshape(signals * 2, 1, 2, tok_rows, channels_all)
    first_angle = 2.0 * np.pi * (np.outer(np.arange(devices), ordering) % classes) / classes
    cos_first = np.cos(first_angle)
    sin_first = np.sin(first_angle)
    full_table = (
        np.stack(
            [np.stack([cos_first, -sin_first], axis=1), np.stack([sin_first, cos_first], axis=1)]
        )
        * norm_factor
    )
    first_table = jnp.asarray(full_table, jnp.float32)
    received = lax.all_to_all(stacked, "ctx", split_axis=3, concat_axis=1, tiled=True)
    channels = received.shape[-1]
    flattened = received.reshape(signals, 2, classes, group_rows * channels)
    time_series = jnp.einsum("qapj,spjx->sqax", first_table, flattened, precision=highest)
    time_series = time_series.reshape(2, devices, group_rows, channels)
    outputs = lax.all_to_all(time_series, "ctx", split_axis=1, concat_axis=1, tiled=True)
    return outputs.reshape(2, tok_rows, channels_all)


def narrow_shards(query_series, key_series, value_series, grad_out, gate_mask, filter_spectrum):
    gating = gate_mask.astype(jnp.float32)[:, None]
    gated_pair = (
        gating * key_series.astype(jnp.float32) * value_series.astype(jnp.float32)
    ).astype(jnp.bfloat16)
    back_signal = (query_series.astype(jnp.float32) * grad_out.astype(jnp.float32)).astype(
        jnp.bfloat16
    )
    series = jnp.stack([gated_pair, back_signal])
    filter_real = filter_spectrum[0]
    filter_imag = filter_spectrum[1]
    combined = forward_spectra(series)[0]
    mirror = partner(combined)
    signal_real = 0.5 * (combined[0] + mirror[0])
    signal_imag = 0.5 * (combined[1] - mirror[1])
    adjoint_real = 0.5 * (combined[1] + mirror[1])
    adjoint_imag = 0.5 * (mirror[0] - combined[0])
    conv_real = signal_real * filter_real - signal_imag * filter_imag
    conv_imag = signal_real * filter_imag + signal_imag * filter_real
    back_real = adjoint_real * filter_real + adjoint_imag * filter_imag
    back_imag = adjoint_imag * filter_real - adjoint_real * filter_imag
    grad_spectrum = jnp.stack(
        [
            adjoint_real * signal_real + adjoint_imag * signal_imag,
            adjoint_imag * signal_real - adjoint_real * signal_imag,
        ]
    )
    minus_pair = jnp.stack([conv_real + back_imag, conv_imag - back_real])
    mirror_back = partner(minus_pair)
    joined = jnp.stack(
        [
            0.5 * (conv_real - back_imag + mirror_back[0]),
            0.5 * (conv_imag + back_real - mirror_back[1]),
        ]
    )
    outputs = inverse_series(joined[None])
    conv_out = outputs[0]
    grad_mixed = outputs[1]
    mixer_out = (query_series.astype(jnp.float32) * conv_out).astype(jnp.bfloat16)
    grad_queries = (grad_out.astype(jnp.float32) * conv_out).astype(jnp.bfloat16)
    grad_keys = (grad_mixed * gating * value_series.astype(jnp.float32)).astype(jnp.bfloat16)
    grad_values = (grad_mixed * gating * key_series.astype(jnp.float32)).astype(jnp.bfloat16)
    return (mixer_out, grad_queries, grad_keys, grad_values, grad_spectrum)


SUB = 16
LANES = 128


def split_table(values):
    exact = np.asarray(values, np.float32)
    high = exact.astype(jnp.bfloat16)
    low = (exact - high.astype(np.float32)).astype(jnp.bfloat16)
    return np.stack([high, low], axis=-3)


def device_tables(devices):
    classes = 2 * devices
    turns = 2.0 * np.pi * (np.outer(np.arange(devices), np.arange(devices)) % classes) / classes
    small = np.stack([np.cos(turns), -np.sin(turns)], axis=1)
    small[0, 1] = np.where(np.arange(devices) % 2 == 0, 1.0, -1.0)
    small = small.reshape(classes, devices)
    full = np.kron(small, np.eye(SUB))
    return split_table(full), split_table(full.T)


def row_tables(devices, rows):
    classes = 2 * devices
    length = classes * rows
    half = rows // 2
    place = np.arange(rows)
    tables = np.zeros((devices, 2, rows, 2, rows))
    for group in range(1, devices):
        freq = group + classes * place
        angle = 2.0 * np.pi * (np.outer(freq, place) % length) / length
        tables[group, 0, :, 0] = np.cos(angle)
        tables[group, 0, :, 1] = np.sin(angle)
        tables[group, 1, :, 0] = -np.sin(angle)
        tables[group, 1, :, 1] = np.cos(angle)
    for part, first in ((0, 0), (1, devices)):
        freq = first + classes * np.arange(half)
        angle = 2.0 * np.pi * (np.outer(freq, place) % length) / length
        tables[0, 0, part * half : (part + 1) * half, part] = np.cos(angle)
        tables[0, 1, part * half : (part + 1) * half, part] = -np.sin(angle)
    tables[0, 1, 0, 0] = np.where(place % 2 == 0, 1.0, -1.0)
    tables = tables.reshape(devices, 2 * rows, 2 * rows) / math.sqrt(length)
    return split_table(tables), split_table(tables.transpose(0, 2, 1))


def fold_tables(rows):
    half = rows // 2
    fold = np.zeros((2, 2, rows, 2, 2, rows))
    spread = np.zeros((2, 2, 2, rows, 2, rows))
    for d in range(rows):
        for part, sign in ((0, 1.0), (1, -1.0)):
            fold[1, part, d, part, 0, d] = 1.0
            fold[1, part, d, part, 1, rows - 1 - d] = sign
            spread[1, part, 0, d, part, d] = 1.0
            spread[1, part, 1, rows - 1 - d, part, d] = sign
    for d in range(half):
        for part, sign in ((0, 1.0), (1, -1.0)):
            if d > 0:
                fold[0, part, d, part, 0, d] = 1.0
                fold[0, part, d, part, 0, rows - d] = sign
                spread[0, part, 0, d, part, d] = 1.0
                spread[0, part, 0, rows - d, part, d] = sign
            fold[0, part, half + d, part, 1, d] = 1.0
            fold[0, part, half + d, part, 1, rows - 1 - d] = sign
            spread[0, part, 1, d, part, half + d] = 1.0
            spread[0, part, 1, rows - 1 - d, part, half + d] = sign
    fold[0, 0, 0, 0, 0, 0] = 1.0
    fold[0, 1, 0, 0, 0, half] = 1.0
    spread[0, 0, 0, 0, 0, 0] = 1.0
    spread[0, 0, 0, half, 1, 0] = 1.0
    return (
        fold.reshape(2, 2 * rows, 4 * rows).astype(jnp.bfloat16),
        spread.reshape(2, 4 * rows, 2 * rows).astype(jnp.bfloat16),
    )


def dot(left, right):
    return jnp.dot(left, right, preferred_element_type=jnp.float32)


def exchange_kernel(
    devices,
    groups,
    rows,
    width,
    gate_ref,
    query_hbm,
    key_hbm,
    value_hbm,
    grad_hbm,
    fold_hbm,
    filter_hbm,
    mix_hbm,
    table_hbm,
    back_hbm,
    unmix_hbm,
    got_grad,
    got_series,
    query_ref,
    key_ref,
    value_ref,
    grad_ref,
    fold_ref,
    filter_ref,
    mix_ref,
    table_ref,
    back_ref,
    unmix_ref,
    send_signal,
    got_signal,
    send_filter,
    got_filter,
    mixed,
    turned,
    send_grad,
    send_series,
    send_sems,
    recv_sems,
    local_sems,
):
    me = lax.axis_index("ctx")
    lane = lax.axis_index("grp")
    barrier = pltpu.get_barrier_semaphore()
    own_fold = jnp.where(me == 0, 0, 1)
    loads = [
        pltpu.make_async_copy(source, target, local_sems.at[2 + at])
        for at, (source, target) in enumerate(
            (
                (query_hbm, query_ref),
                (key_hbm, key_ref),
                (value_hbm, value_ref),
                (grad_hbm, grad_ref),
                (fold_hbm.at[own_fold], fold_ref),
                (filter_hbm, filter_ref),
                (mix_hbm, mix_ref),
                (table_hbm, table_ref),
                (back_hbm, back_ref),
                (unmix_hbm, unmix_ref),
            )
        )
    ]
    for load in loads:
        load.start()

    def greet(step, _):
        pl.semaphore_signal(
            barrier,
            inc=1,
            device_id={"ctx": lax.rem(me + step, devices)},
            device_id_type=pl.DeviceIdType.MESH,
        )
        return 0

    lax.fori_loop(1, devices, greet, 0)
    for step in range(1, groups):
        pl.semaphore_signal(
            barrier,
            inc=1,
            device_id={"grp": lax.rem(lane + step, groups)},
            device_id_type=pl.DeviceIdType.MESH,
        )

    def remote(kind, source, target, step_from, to):
        return pltpu.make_async_remote_copy(
            src_ref=source.at[to],
            dst_ref=target.at[step_from],
            send_sem=send_sems.at[kind, to],
            recv_sem=recv_sems.at[kind, step_from],
            device_id={"ctx": to},
            device_id_type=pl.DeviceIdType.MESH,
        )

    def relay(step, group):
        return pltpu.make_async_remote_copy(
            src_ref=got_filter.at[group],
            dst_ref=got_filter.at[group],
            send_sem=send_sems.at[3 + step, group],
            recv_sem=recv_sems.at[1, group],
            device_id={"grp": lax.rem(lane + step, groups)},
            device_id_type=pl.DeviceIdType.MESH,
        )

    def start_all(kind, source, target):
        def body(step, _):
            remote(kind, source, target, me, lax.rem(me + step, devices)).start()
            return 0

        lax.fori_loop(1, devices, body, 0)

    def wait_received(kind, source, target, first=1):
        def body(step, _):
            other = lax.rem(me + devices - step, devices)
            remote(kind, source, target, other, other).wait_recv()
            return 0

        lax.fori_loop(first, devices, body, 0)

    def wait_sent(kind, source, target):
        def body(step, _):
            remote(kind, source, target, me, lax.rem(me + step, devices)).wait_send()
            return 0

        lax.fori_loop(1, devices, body, 0)

    for load in loads[:4]:
        load.wait()
    gating = gate_ref[...]
    for to in range(devices):
        span = slice(to * width, (to + 1) * width)
        gated = gating * key_ref[:, span].astype(jnp.float32) * value_ref[:, span].astype(jnp.float32)
        back = query_ref[:, span].astype(jnp.float32) * grad_ref[:, span].astype(jnp.float32)
        send_signal[to, 0] = gated.astype(jnp.bfloat16)
        send_signal[to, 1] = back.astype(jnp.bfloat16)
    pl.semaphore_wait(barrier, devices + groups - 2)
    start_all(0, send_signal, got_signal)
    got_signal[me] = send_signal[me]

    for load in loads[4:6]:
        load.wait()
    mine = lax.rem(me, groups) == lane

    @pl.when(mine)
    def _():
        for to in range(devices):
            span = slice(to * width, (to + 1) * width)
            block = filter_ref[:, span]
            high = block.astype(jnp.bfloat16)
            low = (block - high.astype(jnp.float32)).astype(jnp.bfloat16)
            folded = dot(fold_ref[...], high) + dot(fold_ref[...], low)
            send_filter[to] = folded.astype(jnp.bfloat16)
        start_all(1, send_filter, got_filter)
        got_filter[me] = send_filter[me]

    for load in loads[6:]:
        load.wait()
    wait_received(0, send_signal, got_signal)

    def mix(part, _):
        span = pl.ds(pl.multiple_of(part * SUB, SUB), SUB)
        columns = jnp.concatenate(
            [got_signal[:, which, span, :].reshape(devices * SUB, width) for which in (0, 1)], axis=1
        )
        result = dot(mix_ref[0], columns) + dot(mix_ref[1], columns)
        mixed[:, span, :] = result.astype(jnp.bfloat16).reshape(2 * devices, SUB, 2 * width)
        return 0

    lax.fori_loop(0, rows // SUB, mix, 0)

    row_index = lax.broadcasted_iota(jnp.int32, (rows, width), 0)

    def one_group(group):
        source = mixed[pl.ds(2 * group, 2)].reshape(2 * rows, 2 * width)
        spectra = dot(table_ref[group, 0], source) + dot(table_ref[group, 1], source)
        signal_real = spectra[:rows, :width]
        signal_imag = spectra[rows:, :width]
        adjoint_real = spectra[:rows, width:]
        adjoint_imag = spectra[rows:, width:]
        response = got_filter[group].astype(jnp.float32)
        filter_real = response[:rows]
        filter_imag = response[rows:]
        real_pair = jnp.logical_and(row_index == 0, group == 0)

        def times(first_real, first_imag, second_real, second_imag, sign):
            both = first_imag * second_imag
            real = first_real * second_real - jnp.where(real_pair, 0.0, sign * both)
            imag = jnp.where(real_pair, both, first_imag * second_real + sign * first_real * second_imag)
            return real, imag

        grad_real, grad_imag = times(adjoint_real, adjoint_imag, signal_real, signal_imag, -1.0)
        send_grad[group, :rows] = grad_real.astype(jnp.bfloat16)
        send_grad[group, rows:] = grad_imag.astype(jnp.bfloat16)

        @pl.when(group != me)
        def _():
            remote(2, send_grad, got_grad, me, group).start()

        conv_real, conv_imag = times(signal_real, signal_imag, filter_real, filter_imag, 1.0)
        back_real, back_imag = times(adjoint_real, adjoint_imag, filter_real, filter_imag, -1.0)
        product = jnp.concatenate(
            [
                jnp.concatenate([conv_real, back_real], axis=1),
                jnp.concatenate([conv_imag, back_imag], axis=1),
            ],
            axis=0,
        ).astype(jnp.bfloat16)
        result = dot(back_ref[group, 0], product) + dot(back_ref[group, 1], product)
        turned[pl.ds(2 * group, 2)] = result.astype(jnp.bfloat16).reshape(2, rows, 2 * width)

    def in_turn(shift):
        share = lax.rem(lane + shift, groups)

        def body(turn, _):
            place = lax.rem(me // groups + devices // groups - turn, devices // groups)
            group = place * groups + share

            if shift == 0:

                @pl.when(group != me)
                def _():
                    remote(1, send_filter, got_filter, group, group).wait_recv()

                for step in range(1, groups):
                    relay(step, group).start()
            else:
                relay(shift, group).wait_recv()
            one_group(group)
            return 0

        return body

    for shift in range(groups):
        lax.fori_loop(0, devices // groups, in_turn(shift), 0)
    own_grad = pltpu.make_async_copy(send_grad.at[me], got_grad.at[me], local_sems.at[0])
    own_grad.start()

    def unmix(part, _):
        span = pl.ds(pl.multiple_of(part * SUB, SUB), SUB)
        columns = turned[:, span, :].reshape(2 * devices * SUB, 2 * width)
        result = dot(unmix_ref[0], columns) + dot(unmix_ref[1], columns)
        result = result.astype(jnp.bfloat16).reshape(devices, SUB, 2 * width)
        send_series[:, 0, span, :] = result[:, :, :width]
        send_series[:, 1, span, :] = result[:, :, width:]
        return 0

    lax.fori_loop(0, rows // SUB, unmix, 0)
    start_all(3, send_series, got_series)
    own_series = pltpu.make_async_copy(send_series.at[me], got_series.at[me], local_sems.at[1])
    own_series.start()
    own_grad.wait()
    own_series.wait()
    wait_received(2, send_grad, got_grad)
    wait_received(3, send_series, got_series)
    wait_sent(0, send_signal, got_signal)

    @pl.when(mine)
    def _():
        wait_sent(1, send_filter, got_filter)

    def relays_sent(turn, _):
        for step in range(1, groups):
            relay(step, turn * groups + lane).wait_send()
        return 0

    lax.fori_loop(0, devices // groups, relays_sent, 0)
    wait_sent(2, send_grad, got_grad)
    wait_sent(3, send_series, got_series)


def finish_kernel(
    blocks,
    width,
    query_ref,
    key_ref,
    value_ref,
    grad_ref,
    gate_ref,
    spread_ref,
    half_ref,
    series_ref,
    mixer_out,
    queries_out,
    keys_out,
    values_out,
    spectrum_out,
):
    gating = gate_ref[...]
    own_spread = jnp.where(lax.axis_index("ctx") == 0, 0, 1)
    for block in range(blocks):
        span = slice(block * width, (block + 1) * width)
        conv = series_ref[block, 0].astype(jnp.float32)
        back = series_ref[block, 1].astype(jnp.float32) * gating
        mixer_out[:, span] = (query_ref[:, span].astype(jnp.float32) * conv).astype(jnp.bfloat16)
        queries_out[:, span] = (grad_ref[:, span].astype(jnp.float32) * conv).astype(jnp.bfloat16)
        keys_out[:, span] = (back * value_ref[:, span].astype(jnp.float32)).astype(jnp.bfloat16)
        values_out[:, span] = (back * key_ref[:, span].astype(jnp.float32)).astype(jnp.bfloat16)
        spectrum_out[:, span] = dot(spread_ref[own_spread], half_ref[block])


def wide_shards(query_series, key_series, value_series, grad_out, gate_mask, filter_spectrum):
    devices = lax.axis_size("ctx")
    rows, channels = query_series.shape
    width = channels // devices
    gating = gate_mask.astype(jnp.float32)[:, None]
    mix_table, unmix_table = device_tables(devices)
    forward_table, back_table = row_tables(devices, rows)
    folds, spreads = fold_tables(rows)
    groups = lax.axis_size("grp")
    half = jnp.bfloat16
    vmem = pl.BlockSpec(memory_space=pltpu.VMEM)
    anywhere = pl.BlockSpec(memory_space=pl.ANY)
    spectrum_block = (devices, 2 * rows, width)
    series_block = (devices, 2, rows, width)
    got_grad, got_series = pl.pallas_call(
        functools.partial(exchange_kernel, devices, groups, rows, width),
        out_shape=(
            jax.ShapeDtypeStruct(spectrum_block, half),
            jax.ShapeDtypeStruct(series_block, half),
        ),
        in_specs=[vmem] + [anywhere] * 10,
        out_specs=(anywhere, anywhere),
        scratch_shapes=[pltpu.VMEM((rows, channels), half)] * 4
        + [
            pltpu.VMEM((2 * rows, 4 * rows), half),
            pltpu.VMEM((4 * rows, channels), jnp.float32),
            pltpu.VMEM(mix_table.shape, half),
            pltpu.VMEM(forward_table.shape, half),
            pltpu.VMEM(back_table.shape, half),
            pltpu.VMEM(unmix_table.shape, half),
            pltpu.VMEM(series_block, half),
            pltpu.VMEM(series_block, half),
            pltpu.VMEM(spectrum_block, half),
            pltpu.VMEM(spectrum_block, half),
            pltpu.VMEM((2 * devices, rows, 2 * width), half),
            pltpu.VMEM((2 * devices, rows, 2 * width), half),
            pltpu.VMEM(spectrum_block, half),
            pltpu.VMEM(series_block, half),
            pltpu.SemaphoreType.DMA((3 + groups, devices)),
            pltpu.SemaphoreType.DMA((4, devices)),
            pltpu.SemaphoreType.DMA((12,)),
        ],
        compiler_params=pltpu.CompilerParams(
            collective_id=0, has_side_effects=True, vmem_limit_bytes=60 * 1024 * 1024
        ),
        name="exchange",
    )(
        gating,
        query_series,
        key_series,
        value_series,
        grad_out,
        jnp.asarray(folds),
        filter_spectrum.reshape(4 * rows, channels),
        jnp.asarray(mix_table),
        jnp.asarray(forward_table),
        jnp.asarray(back_table),
        jnp.asarray(unmix_table),
    )
    blocks = 2
    columns = pl.BlockSpec((rows, blocks * width), lambda step: (0, step))
    mixer_out, queries, keys, values, spectrum = pl.pallas_call(
        functools.partial(finish_kernel, blocks, width),
        grid=(devices // blocks,),
        out_shape=(jax.ShapeDtypeStruct((rows, channels), half),) * 4
        + (jax.ShapeDtypeStruct((4 * rows, channels), jnp.float32),),
        in_specs=[
            columns,
            columns,
            columns,
            columns,
            pl.BlockSpec((rows, 1), lambda step: (0, 0)),
            pl.BlockSpec((2, 4 * rows, 2 * rows), lambda step: (0, 0, 0)),
            pl.BlockSpec((blocks, 2 * rows, width), lambda step: (step, 0, 0)),
            pl.BlockSpec((blocks, 2, rows, width), lambda step: (step, 0, 0, 0)),
        ],
        out_specs=(columns,) * 4 + (pl.BlockSpec((4 * rows, blocks * width), lambda step: (0, step)),),
        compiler_params=pltpu.CompilerParams(vmem_limit_bytes=60 * 1024 * 1024),
        name="finish",
    )(query_series, key_series, value_series, grad_out, gating, jnp.asarray(spreads), got_grad, got_series)
    return mixer_out, queries, keys, values, spectrum.reshape(2, 2, rows, channels)


def shards(query_series, *others):
    devices = lax.axis_size("ctx")
    rows, channels = query_series.shape
    if rows % SUB == 0 and channels % (devices * LANES) == 0 and devices % lax.axis_size("grp") == 0:
        return wide_shards(query_series, *others)
    return narrow_shards(query_series, *others)


def solution(mesh):
    placed = (
        P(("grp", "ctx"), None),
        P(("grp", "ctx"), None),
        P(("grp", "ctx"), None),
        P(("grp", "ctx"), None),
        P(("grp", "ctx")),
        P(None, "ctx", None, None),
    )
    return jax.shard_map(
        shards,
        mesh=mesh,
        in_specs=placed,
        out_specs=(
            P(("grp", "ctx"), None),
            P(("grp", "ctx"), None),
            P(("grp", "ctx"), None),
            P(("grp", "ctx"), None),
            P(None, ("grp", "ctx"), None, None),
        ),
        check_vma=False,
    )
```

```python
import functools
import math

import jax
import jax.numpy as jnp
import numpy as np
from jax import lax
from jax.experimental import pallas as pl
from jax.experimental.pallas import tpu as pltpu
from jax.sharding import PartitionSpec as P

highest = lax.Precision.HIGHEST


def class_order(devices):
    indices = np.arange(2 * devices)
    pair_index = indices // 2
    parity = indices % 2
    return np.where(
        pair_index == 0,
        parity * devices,
        np.where(parity == 0, pair_index, 2 * devices - pair_index),
    )


def partner(spectrum):
    flipped = jnp.flip(spectrum, axis=-2)
    crossed = jnp.flip(flipped, axis=-3)
    anchor_head = jnp.roll(flipped[..., 0:1, :, :], 1, axis=-2)
    anchor = jnp.concatenate([anchor_head, flipped[..., 1:2, :, :]], axis=-3)
    return jnp.where(lax.axis_index("ctx") == 0, anchor, crossed)


def forward_spectra(series):
    devices = lax.axis_size("ctx")
    tok_rows = series.shape[1]
    group_rows = tok_rows // devices
    classes = 2 * devices
    fft_length = classes * tok_rows
    ordering = class_order(devices)
    norm_factor = 1.0 / math.sqrt(fft_length)
    positions = lax.axis_index("ctx") * group_rows + jnp.arange(group_rows, dtype=jnp.int32)
    offsets = jnp.arange(devices, dtype=jnp.int32) * tok_rows
    order_column = jnp.asarray(ordering, jnp.int32)[:, None, None]
    first_turns = order_column * (offsets[None, :, None] + positions[None, None, :]) % fft_length
    first_angle = first_turns.astype(jnp.float32) * (-2.0 * math.pi / fft_length)
    first_table = jnp.stack([jnp.cos(first_angle), jnp.sin(first_angle)])
    rows_index = np.arange(tok_rows)
    second_angle = 2.0 * np.pi * (np.outer(rows_index, rows_index) % tok_rows) / tok_rows
    cos_second = np.cos(second_angle)
    sin_second = -np.sin(second_angle)
    row_real = np.stack([cos_second, -sin_second], axis=1)
    row_imag = np.stack([sin_second, cos_second], axis=1)
    second_table = jnp.asarray(np.stack([row_real, row_imag]) * norm_factor, jnp.float32)
    shaped = series.reshape(2, devices, group_rows, series.shape[-1])
    received = lax.all_to_all(shaped, "ctx", split_axis=1, concat_axis=1, tiled=True)
    channels = received.shape[-1]
    widened = received.astype(jnp.float32)
    parts = jnp.einsum("qjab,sabx->sqjbx", first_table, widened, precision=highest)
    parts = jnp.stack([parts[0, 0] - parts[1, 1], parts[0, 1] + parts[1, 0]])[None]
    signals = parts.shape[0]
    stacked = parts.reshape(signals * 2, devices, 2, group_rows, channels)
    received = lax.all_to_all(stacked, "ctx", split_axis=1, concat_axis=3, tiled=True)
    channels = received.shape[-1]
    signals = received.shape[0] // 2
    shaped = received.reshape(signals, 2, 2, tok_rows, channels)
    joined = jnp.einsum("qdpb,speby->sqedy", second_table, shaped, precision=highest)
    spectrum = joined.reshape(signals * 2, 2, tok_rows, channels)
    return spectrum.reshape(spectrum.shape[0] // 2, 2, 2, tok_rows, series.shape[-1])


def inverse_series(spectra):
    devices = lax.axis_size("ctx")
    signals = spectra.shape[0]
    tok_rows = spectra.shape[3]
    channels_all = spectra.shape[4]
    group_rows = tok_rows // devices
    classes = 2 * devices
    fft_length = classes * tok_rows
    ordering = class_order(devices)
    norm_factor = 1.0 / math.sqrt(fft_length)
    location = lax.axis_index("ctx")
    own_classes = jnp.stack(
        [
            jnp.where(location == 0, 0, location),
            jnp.where(location == 0, devices, classes - location),
        ]
    )
    rows_index = jnp.arange(tok_rows, dtype=jnp.int32)
    square_turns = rows_index[:, None] * rows_index[None, :] * classes % fft_length
    second_turns = (
        square_turns[None, :, :] + own_classes[:, None, None] * rows_index[None, :, None]
    ) % fft_length
    second_angle = second_turns.astype(jnp.float32) * (2.0 * math.pi / fft_length)
    cos_second = jnp.cos(second_angle)
    sin_second = jnp.sin(second_angle)
    second_table = jnp.stack(
        [jnp.stack([cos_second, -sin_second], axis=2), jnp.stack([sin_second, cos_second], axis=2)],
        axis=1,
    )
    stacked = jnp.einsum("eqbpd,spedy->sqeby", second_table, spectra, precision=highest)
    stacked = stacked.reshape(signals * 2, 1, 2, tok_rows, channels_all)
    first_angle = 2.0 * np.pi * (np.outer(np.arange(devices), ordering) % classes) / classes
    cos_first = np.cos(first_angle)
    sin_first = np.sin(first_angle)
    full_table = (
        np.stack(
            [np.stack([cos_first, -sin_first], axis=1), np.stack([sin_first, cos_first], axis=1)]
        )
        * norm_factor
    )
    first_table = jnp.asarray(full_table, jnp.float32)
    received = lax.all_to_all(stacked, "ctx", split_axis=3, concat_axis=1, tiled=True)
    channels = received.shape[-1]
    flattened = received.reshape(signals, 2, classes, group_rows * channels)
    time_series = jnp.einsum("qapj,spjx->sqax", first_table, flattened, precision=highest)
    time_series = time_series.reshape(2, devices, group_rows, channels)
    outputs = lax.all_to_all(time_series, "ctx", split_axis=1, concat_axis=1, tiled=True)
    return outputs.reshape(2, tok_rows, channels_all)


def narrow_shards(query_series, key_series, value_series, grad_out, gate_mask, filter_spectrum):
    gating = gate_mask.astype(jnp.float32)[:, None]
    gated_pair = (
        gating * key_series.astype(jnp.float32) * value_series.astype(jnp.float32)
    ).astype(jnp.bfloat16)
    back_signal = (query_series.astype(jnp.float32) * grad_out.astype(jnp.float32)).astype(
        jnp.bfloat16
    )
    series = jnp.stack([gated_pair, back_signal])
    filter_real = filter_spectrum[0]
    filter_imag = filter_spectrum[1]
    combined = forward_spectra(series)[0]
    mirror = partner(combined)
    signal_real = 0.5 * (combined[0] + mirror[0])
    signal_imag = 0.5 * (combined[1] - mirror[1])
    adjoint_real = 0.5 * (combined[1] + mirror[1])
    adjoint_imag = 0.5 * (mirror[0] - combined[0])
    conv_real = signal_real * filter_real - signal_imag * filter_imag
    conv_imag = signal_real * filter_imag + signal_imag * filter_real
    back_real = adjoint_real * filter_real + adjoint_imag * filter_imag
    back_imag = adjoint_imag * filter_real - adjoint_real * filter_imag
    grad_spectrum = jnp.stack(
        [
            adjoint_real * signal_real + adjoint_imag * signal_imag,
            adjoint_imag * signal_real - adjoint_real * signal_imag,
        ]
    )
    minus_pair = jnp.stack([conv_real + back_imag, conv_imag - back_real])
    mirror_back = partner(minus_pair)
    joined = jnp.stack(
        [
            0.5 * (conv_real - back_imag + mirror_back[0]),
            0.5 * (conv_imag + back_real - mirror_back[1]),
        ]
    )
    outputs = inverse_series(joined[None])
    conv_out = outputs[0]
    grad_mixed = outputs[1]
    mixer_out = (query_series.astype(jnp.float32) * conv_out).astype(jnp.bfloat16)
    grad_queries = (grad_out.astype(jnp.float32) * conv_out).astype(jnp.bfloat16)
    grad_keys = (grad_mixed * gating * value_series.astype(jnp.float32)).astype(jnp.bfloat16)
    grad_values = (grad_mixed * gating * key_series.astype(jnp.float32)).astype(jnp.bfloat16)
    return (mixer_out, grad_queries, grad_keys, grad_values, grad_spectrum)


SUB = 16
LANES = 128


def split_table(values):
    exact = np.asarray(values, np.float32)
    high = exact.astype(jnp.bfloat16)
    low = (exact - high.astype(np.float32)).astype(jnp.bfloat16)
    return np.stack([high, low], axis=-3)


def device_tables(devices):
    classes = 2 * devices
    turns = 2.0 * np.pi * (np.outer(np.arange(devices), np.arange(devices)) % classes) / classes
    small = np.stack([np.cos(turns), -np.sin(turns)], axis=1)
    small[0, 1] = np.where(np.arange(devices) % 2 == 0, 1.0, -1.0)
    small = small.reshape(classes, devices)
    full = np.kron(small, np.eye(SUB))
    return split_table(full), split_table(full.T)


def row_tables(devices, rows):
    classes = 2 * devices
    length = classes * rows
    half = rows // 2
    place = np.arange(rows)
    tables = np.zeros((devices, 2, rows, 2, rows))
    for group in range(1, devices):
        freq = group + classes * place
        angle = 2.0 * np.pi * (np.outer(freq, place) % length) / length
        tables[group, 0, :, 0] = np.cos(angle)
        tables[group, 0, :, 1] = np.sin(angle)
        tables[group, 1, :, 0] = -np.sin(angle)
        tables[group, 1, :, 1] = np.cos(angle)
    for part, first in ((0, 0), (1, devices)):
        freq = first + classes * np.arange(half)
        angle = 2.0 * np.pi * (np.outer(freq, place) % length) / length
        tables[0, 0, part * half : (part + 1) * half, part] = np.cos(angle)
        tables[0, 1, part * half : (part + 1) * half, part] = -np.sin(angle)
    tables[0, 1, 0, 0] = np.where(place % 2 == 0, 1.0, -1.0)
    tables = tables.reshape(devices, 2 * rows, 2 * rows) / math.sqrt(length)
    return split_table(tables), split_table(tables.transpose(0, 2, 1))


def fold_tables(rows):
    half = rows // 2
    fold = np.zeros((2, 2, rows, 2, 2, rows))
    spread = np.zeros((2, 2, 2, rows, 2, rows))
    for d in range(rows):
        for part, sign in ((0, 1.0), (1, -1.0)):
            fold[1, part, d, part, 0, d] = 1.0
            fold[1, part, d, part, 1, rows - 1 - d] = sign
            spread[1, part, 0, d, part, d] = 1.0
            spread[1, part, 1, rows - 1 - d, part, d] = sign
    for d in range(half):
        for part, sign in ((0, 1.0), (1, -1.0)):
            if d > 0:
                fold[0, part, d, part, 0, d] = 1.0
                fold[0, part, d, part, 0, rows - d] = sign
                spread[0, part, 0, d, part, d] = 1.0
                spread[0, part, 0, rows - d, part, d] = sign
            fold[0, part, half + d, part, 1, d] = 1.0
            fold[0, part, half + d, part, 1, rows - 1 - d] = sign
            spread[0, part, 1, d, part, half + d] = 1.0
            spread[0, part, 1, rows - 1 - d, part, half + d] = sign
    fold[0, 0, 0, 0, 0, 0] = 1.0
    fold[0, 1, 0, 0, 0, half] = 1.0
    spread[0, 0, 0, 0, 0, 0] = 1.0
    spread[0, 0, 0, half, 1, 0] = 1.0
    return (
        fold.reshape(2, 2 * rows, 4 * rows).astype(jnp.bfloat16),
        spread.reshape(2, 4 * rows, 2 * rows).astype(jnp.bfloat16),
    )


def dot(left, right):
    return jnp.dot(left, right, preferred_element_type=jnp.float32)


def gate_column(mask):
    rows = mask.shape[1]
    across = lax.broadcasted_iota(jnp.int32, (rows, rows), 1)
    down = lax.broadcasted_iota(jnp.int32, (rows, rows), 0)
    spots = jnp.where(across == down, mask.astype(jnp.float32), 0.0)
    return jnp.sum(spots, axis=1, keepdims=True)


def exchange_kernel(
    devices,
    groups,
    rows,
    width,
    gate_ref,
    query_hbm,
    key_hbm,
    value_hbm,
    grad_hbm,
    fold_hbm,
    filter_hbm,
    mix_hbm,
    table_hbm,
    back_hbm,
    unmix_hbm,
    got_grad,
    got_series,
    query_ref,
    key_ref,
    value_ref,
    grad_ref,
    fold_ref,
    filter_ref,
    mix_ref,
    table_ref,
    back_ref,
    unmix_ref,
    send_signal,
    got_signal,
    send_filter,
    got_filter,
    mixed,
    turned,
    send_grad,
    send_series,
    send_sems,
    recv_sems,
    local_sems,
):
    me = lax.axis_index("ctx")
    lane = lax.axis_index("grp")
    barrier = pltpu.get_barrier_semaphore()
    own_fold = jnp.where(me == 0, 0, 1)
    loads = [
        pltpu.make_async_copy(source, target, local_sems.at[2 + at])
        for at, (source, target) in enumerate(
            (
                (query_hbm, query_ref),
                (key_hbm, key_ref),
                (value_hbm, value_ref),
                (grad_hbm, grad_ref),
                (fold_hbm.at[own_fold], fold_ref),
                (filter_hbm, filter_ref),
                (mix_hbm, mix_ref),
                (table_hbm, table_ref),
                (back_hbm, back_ref),
                (unmix_hbm, unmix_ref),
            )
        )
    ]
    for load in loads:
        load.start()

    def greet(step, _):
        pl.semaphore_signal(
            barrier,
            inc=1,
            device_id={"ctx": lax.rem(me + step, devices)},
            device_id_type=pl.DeviceIdType.MESH,
        )
        return 0

    lax.fori_loop(1, devices, greet, 0)
    for step in range(1, groups):
        pl.semaphore_signal(
            barrier,
            inc=1,
            device_id={"grp": lax.rem(lane + step, groups)},
            device_id_type=pl.DeviceIdType.MESH,
        )

    near = devices // 2
    side = me // near
    spot = lax.rem(me, near)

    def partner_at(step, direction):
        step = step + step // near
        half_at = lax.rem(side + 1 + step // near, 2)
        return half_at * near + lax.rem(spot + near + direction * lax.rem(step, near), near)

    def remote(kind, source, target, step_from, to):
        return pltpu.make_async_remote_copy(
            src_ref=source.at[to],
            dst_ref=target.at[step_from],
            send_sem=send_sems.at[kind, to],
            recv_sem=recv_sems.at[kind, step_from],
            device_id={"ctx": to},
            device_id_type=pl.DeviceIdType.MESH,
        )

    def relay(step, group):
        return pltpu.make_async_remote_copy(
            src_ref=got_filter.at[group],
            dst_ref=got_filter.at[group],
            send_sem=send_sems.at[3 + step, group],
            recv_sem=recv_sems.at[1, group],
            device_id={"grp": lax.rem(lane + step, groups)},
            device_id_type=pl.DeviceIdType.MESH,
        )

    def start_all(kind, source, target):
        def body(step, _):
            remote(kind, source, target, me, partner_at(step, 1)).start()
            return 0

        lax.fori_loop(0, devices - 1, body, 0)

    def wait_received(kind, source, target):
        def body(step, _):
            other = partner_at(step, -1)
            remote(kind, source, target, other, other).wait_recv()
            return 0

        lax.fori_loop(0, devices - 1, body, 0)

    def wait_sent(kind, source, target):
        def body(step, _):
            remote(kind, source, target, me, partner_at(step, 1)).wait_send()
            return 0

        lax.fori_loop(0, devices - 1, body, 0)

    for load in loads[:4]:
        load.wait()
    gating = gate_column(gate_ref[...])
    for to in range(devices):
        span = slice(to * width, (to + 1) * width)
        gated = gating * key_ref[:, span].astype(jnp.float32) * value_ref[:, span].astype(jnp.float32)
        back = query_ref[:, span].astype(jnp.float32) * grad_ref[:, span].astype(jnp.float32)
        send_signal[to, 0] = gated.astype(jnp.bfloat16)
        send_signal[to, 1] = back.astype(jnp.bfloat16)
    pl.semaphore_wait(barrier, devices + groups - 2)
    start_all(0, send_signal, got_signal)
    got_signal[me] = send_signal[me]

    for load in loads[4:6]:
        load.wait()
    mine = lax.rem(me, groups) == lane

    @pl.when(mine)
    def _():
        for to in range(devices):
            span = slice(to * width, (to + 1) * width)
            block = filter_ref[:, span]
            high = block.astype(jnp.bfloat16)
            low = (block - high.astype(jnp.float32)).astype(jnp.bfloat16)
            folded = dot(fold_ref[...], high) + dot(fold_ref[...], low)
            send_filter[to] = folded.astype(jnp.bfloat16)
        start_all(1, send_filter, got_filter)
        got_filter[me] = send_filter[me]

    for load in loads[6:]:
        load.wait()
    wait_received(0, send_signal, got_signal)

    def mix(part, _):
        span = pl.ds(pl.multiple_of(part * SUB, SUB), SUB)
        columns = jnp.concatenate(
            [got_signal[:, which, span, :].reshape(devices * SUB, width) for which in (0, 1)], axis=1
        )
        result = dot(mix_ref[0], columns) + dot(mix_ref[1], columns)
        mixed[:, span, :] = result.astype(jnp.bfloat16).reshape(2 * devices, SUB, 2 * width)
        return 0

    lax.fori_loop(0, rows // SUB, mix, 0)

    row_index = lax.broadcasted_iota(jnp.int32, (rows, width), 0)

    def one_group(group):
        source = mixed[pl.ds(2 * group, 2)].reshape(2 * rows, 2 * width)
        spectra = dot(table_ref[group, 0], source) + dot(table_ref[group, 1], source)
        signal_real = spectra[:rows, :width]
        signal_imag = spectra[rows:, :width]
        adjoint_real = spectra[:rows, width:]
        adjoint_imag = spectra[rows:, width:]
        response = got_filter[group].astype(jnp.float32)
        filter_real = response[:rows]
        filter_imag = response[rows:]
        real_pair = jnp.logical_and(row_index == 0, group == 0)

        def times(first_real, first_imag, second_real, second_imag, sign):
            both = first_imag * second_imag
            real = first_real * second_real - jnp.where(real_pair, 0.0, sign * both)
            imag = jnp.where(real_pair, both, first_imag * second_real + sign * first_real * second_imag)
            return real, imag

        grad_real, grad_imag = times(adjoint_real, adjoint_imag, signal_real, signal_imag, -1.0)
        send_grad[group, :rows] = grad_real.astype(jnp.bfloat16)
        send_grad[group, rows:] = grad_imag.astype(jnp.bfloat16)

        @pl.when(group != me)
        def _():
            remote(2, send_grad, got_grad, me, group).start()

        conv_real, conv_imag = times(signal_real, signal_imag, filter_real, filter_imag, 1.0)
        back_real, back_imag = times(adjoint_real, adjoint_imag, filter_real, filter_imag, -1.0)
        product = jnp.concatenate(
            [
                jnp.concatenate([conv_real, back_real], axis=1),
                jnp.concatenate([conv_imag, back_imag], axis=1),
            ],
            axis=0,
        ).astype(jnp.bfloat16)
        result = dot(back_ref[group, 0], product) + dot(back_ref[group, 1], product)
        turned[pl.ds(2 * group, 2)] = result.astype(jnp.bfloat16).reshape(2, rows, 2 * width)

    turns = near // groups

    def in_turn(shift):
        share = lax.rem(lane + shift, groups)

        def body(turn, _):
            half_at = lax.rem(side + 1 + turn // turns, 2)
            place = lax.rem(spot // groups + turns - lax.rem(turn, turns), turns)
            group = half_at * near + place * groups + share

            if shift == 0:

                @pl.when(group != me)
                def _():
                    remote(1, send_filter, got_filter, group, group).wait_recv()

                for step in range(1, groups):
                    relay(step, group).start()
            else:
                relay(shift, group).wait_recv()
            one_group(group)
            return 0

        return body

    for shift in range(groups):
        lax.fori_loop(0, devices // groups, in_turn(shift), 0)
    own_grad = pltpu.make_async_copy(send_grad.at[me], got_grad.at[me], local_sems.at[0])
    own_grad.start()

    def unmix(part, _):
        span = pl.ds(pl.multiple_of(part * SUB, SUB), SUB)
        columns = turned[:, span, :].reshape(2 * devices * SUB, 2 * width)
        result = dot(unmix_ref[0], columns) + dot(unmix_ref[1], columns)
        result = result.astype(jnp.bfloat16).reshape(devices, SUB, 2 * width)
        send_series[:, 0, span, :] = result[:, :, :width]
        send_series[:, 1, span, :] = result[:, :, width:]
        return 0

    lax.fori_loop(0, rows // SUB, unmix, 0)
    start_all(3, send_series, got_series)
    own_series = pltpu.make_async_copy(send_series.at[me], got_series.at[me], local_sems.at[1])
    own_series.start()
    own_grad.wait()
    own_series.wait()
    wait_received(2, send_grad, got_grad)
    wait_received(3, send_series, got_series)
    wait_sent(0, send_signal, got_signal)

    @pl.when(mine)
    def _():
        wait_sent(1, send_filter, got_filter)

    def relays_sent(turn, _):
        for step in range(1, groups):
            relay(step, turn * groups + lane).wait_send()
        return 0

    lax.fori_loop(0, devices // groups, relays_sent, 0)
    wait_sent(2, send_grad, got_grad)
    wait_sent(3, send_series, got_series)


def finish_kernel(
    blocks,
    width,
    query_ref,
    key_ref,
    value_ref,
    grad_ref,
    gate_ref,
    spread_ref,
    half_ref,
    series_ref,
    mixer_out,
    queries_out,
    keys_out,
    values_out,
    spectrum_out,
):
    gating = gate_column(gate_ref[...])
    own_spread = jnp.where(lax.axis_index("ctx") == 0, 0, 1)
    for block in range(blocks):
        span = slice(block * width, (block + 1) * width)
        conv = series_ref[block, 0].astype(jnp.float32)
        back = series_ref[block, 1].astype(jnp.float32) * gating
        mixer_out[:, span] = (query_ref[:, span].astype(jnp.float32) * conv).astype(jnp.bfloat16)
        queries_out[:, span] = (grad_ref[:, span].astype(jnp.float32) * conv).astype(jnp.bfloat16)
        keys_out[:, span] = (back * value_ref[:, span].astype(jnp.float32)).astype(jnp.bfloat16)
        values_out[:, span] = (back * key_ref[:, span].astype(jnp.float32)).astype(jnp.bfloat16)
        spectrum_out[:, span] = dot(spread_ref[own_spread], half_ref[block])


def wide_shards(query_series, key_series, value_series, grad_out, gate_mask, filter_spectrum):
    devices = lax.axis_size("ctx")
    rows, channels = query_series.shape
    width = channels // devices
    gating = gate_mask[None, :]
    mix_table, unmix_table = device_tables(devices)
    forward_table, back_table = row_tables(devices, rows)
    folds, spreads = fold_tables(rows)
    groups = lax.axis_size("grp")
    half = jnp.bfloat16
    vmem = pl.BlockSpec(memory_space=pltpu.VMEM)
    anywhere = pl.BlockSpec(memory_space=pl.ANY)
    spectrum_block = (devices, 2 * rows, width)
    series_block = (devices, 2, rows, width)
    got_grad, got_series = pl.pallas_call(
        functools.partial(exchange_kernel, devices, groups, rows, width),
        out_shape=(
            jax.ShapeDtypeStruct(spectrum_block, half),
            jax.ShapeDtypeStruct(series_block, half),
        ),
        in_specs=[vmem] + [anywhere] * 10,
        out_specs=(anywhere, anywhere),
        scratch_shapes=[pltpu.VMEM((rows, channels), half)] * 4
        + [
            pltpu.VMEM((2 * rows, 4 * rows), half),
            pltpu.VMEM((4 * rows, channels), jnp.float32),
            pltpu.VMEM(mix_table.shape, half),
            pltpu.VMEM(forward_table.shape, half),
            pltpu.VMEM(back_table.shape, half),
            pltpu.VMEM(unmix_table.shape, half),
            pltpu.VMEM(series_block, half),
            pltpu.VMEM(series_block, half),
            pltpu.VMEM(spectrum_block, half),
            pltpu.VMEM(spectrum_block, half),
            pltpu.VMEM((2 * devices, rows, 2 * width), half),
            pltpu.VMEM((2 * devices, rows, 2 * width), half),
            pltpu.VMEM(spectrum_block, half),
            pltpu.VMEM(series_block, half),
            pltpu.SemaphoreType.DMA((3 + groups, devices)),
            pltpu.SemaphoreType.DMA((4, devices)),
            pltpu.SemaphoreType.DMA((12,)),
        ],
        compiler_params=pltpu.CompilerParams(
            collective_id=0, has_side_effects=True, vmem_limit_bytes=60 * 1024 * 1024
        ),
        name="exchange",
    )(
        gating,
        query_series,
        key_series,
        value_series,
        grad_out,
        jnp.asarray(folds),
        filter_spectrum.reshape(4 * rows, channels),
        jnp.asarray(mix_table),
        jnp.asarray(forward_table),
        jnp.asarray(back_table),
        jnp.asarray(unmix_table),
    )
    blocks = 2
    columns = pl.BlockSpec((rows, blocks * width), lambda step: (0, step))
    mixer_out, queries, keys, values, spectrum = pl.pallas_call(
        functools.partial(finish_kernel, blocks, width),
        grid=(devices // blocks,),
        out_shape=(jax.ShapeDtypeStruct((rows, channels), half),) * 4
        + (jax.ShapeDtypeStruct((4 * rows, channels), jnp.float32),),
        in_specs=[
            columns,
            columns,
            columns,
            columns,
            pl.BlockSpec((1, rows), lambda step: (0, 0)),
            pl.BlockSpec((2, 4 * rows, 2 * rows), lambda step: (0, 0, 0)),
            pl.BlockSpec((blocks, 2 * rows, width), lambda step: (step, 0, 0)),
            pl.BlockSpec((blocks, 2, rows, width), lambda step: (step, 0, 0, 0)),
        ],
        out_specs=(columns,) * 4 + (pl.BlockSpec((4 * rows, blocks * width), lambda step: (0, step)),),
        compiler_params=pltpu.CompilerParams(vmem_limit_bytes=32 * 1024 * 1024),
        name="finish",
    )(query_series, key_series, value_series, grad_out, gating, jnp.asarray(spreads), got_grad, got_series)
    return mixer_out, queries, keys, values, spectrum.reshape(2, 2, rows, channels)


def shards(query_series, *others):
    devices = lax.axis_size("ctx")
    rows, channels = query_series.shape
    if rows % SUB == 0 and channels % (devices * LANES) == 0 and devices % (2 * lax.axis_size("grp")) == 0:
        return wide_shards(query_series, *others)
    return narrow_shards(query_series, *others)


def solution(mesh):
    placed = (
        P(("grp", "ctx"), None),
        P(("grp", "ctx"), None),
        P(("grp", "ctx"), None),
        P(("grp", "ctx"), None),
        P(("grp", "ctx")),
        P(None, "ctx", None, None),
    )
    return jax.shard_map(
        shards,
        mesh=mesh,
        in_specs=placed,
        out_specs=(
            P(("grp", "ctx"), None),
            P(("grp", "ctx"), None),
            P(("grp", "ctx"), None),
            P(("grp", "ctx"), None),
            P(None, ("grp", "ctx"), None, None),
        ),
        check_vma=False,
    )
```

```python
import functools
import math

import jax
import jax.numpy as jnp
import numpy as np
from jax import lax
from jax.experimental import pallas as pl
from jax.experimental.pallas import tpu as pltpu
from jax.sharding import PartitionSpec as P

highest = lax.Precision.HIGHEST


def class_order(devices):
    indices = np.arange(2 * devices)
    pair_index = indices // 2
    parity = indices % 2
    return np.where(
        pair_index == 0,
        parity * devices,
        np.where(parity == 0, pair_index, 2 * devices - pair_index),
    )


def partner(spectrum):
    flipped = jnp.flip(spectrum, axis=-2)
    crossed = jnp.flip(flipped, axis=-3)
    anchor_head = jnp.roll(flipped[..., 0:1, :, :], 1, axis=-2)
    anchor = jnp.concatenate([anchor_head, flipped[..., 1:2, :, :]], axis=-3)
    return jnp.where(lax.axis_index("ctx") == 0, anchor, crossed)


def forward_spectra(series):
    devices = lax.axis_size("ctx")
    tok_rows = series.shape[1]
    group_rows = tok_rows // devices
    classes = 2 * devices
    fft_length = classes * tok_rows
    ordering = class_order(devices)
    norm_factor = 1.0 / math.sqrt(fft_length)
    positions = lax.axis_index("ctx") * group_rows + jnp.arange(group_rows, dtype=jnp.int32)
    offsets = jnp.arange(devices, dtype=jnp.int32) * tok_rows
    order_column = jnp.asarray(ordering, jnp.int32)[:, None, None]
    first_turns = order_column * (offsets[None, :, None] + positions[None, None, :]) % fft_length
    first_angle = first_turns.astype(jnp.float32) * (-2.0 * math.pi / fft_length)
    first_table = jnp.stack([jnp.cos(first_angle), jnp.sin(first_angle)])
    rows_index = np.arange(tok_rows)
    second_angle = 2.0 * np.pi * (np.outer(rows_index, rows_index) % tok_rows) / tok_rows
    cos_second = np.cos(second_angle)
    sin_second = -np.sin(second_angle)
    row_real = np.stack([cos_second, -sin_second], axis=1)
    row_imag = np.stack([sin_second, cos_second], axis=1)
    second_table = jnp.asarray(np.stack([row_real, row_imag]) * norm_factor, jnp.float32)
    shaped = series.reshape(2, devices, group_rows, series.shape[-1])
    received = lax.all_to_all(shaped, "ctx", split_axis=1, concat_axis=1, tiled=True)
    channels = received.shape[-1]
    widened = received.astype(jnp.float32)
    parts = jnp.einsum("qjab,sabx->sqjbx", first_table, widened, precision=highest)
    parts = jnp.stack([parts[0, 0] - parts[1, 1], parts[0, 1] + parts[1, 0]])[None]
    signals = parts.shape[0]
    stacked = parts.reshape(signals * 2, devices, 2, group_rows, channels)
    received = lax.all_to_all(stacked, "ctx", split_axis=1, concat_axis=3, tiled=True)
    channels = received.shape[-1]
    signals = received.shape[0] // 2
    shaped = received.reshape(signals, 2, 2, tok_rows, channels)
    joined = jnp.einsum("qdpb,speby->sqedy", second_table, shaped, precision=highest)
    spectrum = joined.reshape(signals * 2, 2, tok_rows, channels)
    return spectrum.reshape(spectrum.shape[0] // 2, 2, 2, tok_rows, series.shape[-1])


def inverse_series(spectra):
    devices = lax.axis_size("ctx")
    signals = spectra.shape[0]
    tok_rows = spectra.shape[3]
    channels_all = spectra.shape[4]
    group_rows = tok_rows // devices
    classes = 2 * devices
    fft_length = classes * tok_rows
    ordering = class_order(devices)
    norm_factor = 1.0 / math.sqrt(fft_length)
    location = lax.axis_index("ctx")
    own_classes = jnp.stack(
        [
            jnp.where(location == 0, 0, location),
            jnp.where(location == 0, devices, classes - location),
        ]
    )
    rows_index = jnp.arange(tok_rows, dtype=jnp.int32)
    square_turns = rows_index[:, None] * rows_index[None, :] * classes % fft_length
    second_turns = (
        square_turns[None, :, :] + own_classes[:, None, None] * rows_index[None, :, None]
    ) % fft_length
    second_angle = second_turns.astype(jnp.float32) * (2.0 * math.pi / fft_length)
    cos_second = jnp.cos(second_angle)
    sin_second = jnp.sin(second_angle)
    second_table = jnp.stack(
        [jnp.stack([cos_second, -sin_second], axis=2), jnp.stack([sin_second, cos_second], axis=2)],
        axis=1,
    )
    stacked = jnp.einsum("eqbpd,spedy->sqeby", second_table, spectra, precision=highest)
    stacked = stacked.reshape(signals * 2, 1, 2, tok_rows, channels_all)
    first_angle = 2.0 * np.pi * (np.outer(np.arange(devices), ordering) % classes) / classes
    cos_first = np.cos(first_angle)
    sin_first = np.sin(first_angle)
    full_table = (
        np.stack(
            [np.stack([cos_first, -sin_first], axis=1), np.stack([sin_first, cos_first], axis=1)]
        )
        * norm_factor
    )
    first_table = jnp.asarray(full_table, jnp.float32)
    received = lax.all_to_all(stacked, "ctx", split_axis=3, concat_axis=1, tiled=True)
    channels = received.shape[-1]
    flattened = received.reshape(signals, 2, classes, group_rows * channels)
    time_series = jnp.einsum("qapj,spjx->sqax", first_table, flattened, precision=highest)
    time_series = time_series.reshape(2, devices, group_rows, channels)
    outputs = lax.all_to_all(time_series, "ctx", split_axis=1, concat_axis=1, tiled=True)
    return outputs.reshape(2, tok_rows, channels_all)


def narrow_shards(query_series, key_series, value_series, grad_out, gate_mask, filter_spectrum):
    gating = gate_mask.astype(jnp.float32)[:, None]
    gated_pair = (
        gating * key_series.astype(jnp.float32) * value_series.astype(jnp.float32)
    ).astype(jnp.bfloat16)
    back_signal = (query_series.astype(jnp.float32) * grad_out.astype(jnp.float32)).astype(
        jnp.bfloat16
    )
    series = jnp.stack([gated_pair, back_signal])
    filter_real = filter_spectrum[0]
    filter_imag = filter_spectrum[1]
    combined = forward_spectra(series)[0]
    mirror = partner(combined)
    signal_real = 0.5 * (combined[0] + mirror[0])
    signal_imag = 0.5 * (combined[1] - mirror[1])
    adjoint_real = 0.5 * (combined[1] + mirror[1])
    adjoint_imag = 0.5 * (mirror[0] - combined[0])
    conv_real = signal_real * filter_real - signal_imag * filter_imag
    conv_imag = signal_real * filter_imag + signal_imag * filter_real
    back_real = adjoint_real * filter_real + adjoint_imag * filter_imag
    back_imag = adjoint_imag * filter_real - adjoint_real * filter_imag
    grad_spectrum = jnp.stack(
        [
            adjoint_real * signal_real + adjoint_imag * signal_imag,
            adjoint_imag * signal_real - adjoint_real * signal_imag,
        ]
    )
    minus_pair = jnp.stack([conv_real + back_imag, conv_imag - back_real])
    mirror_back = partner(minus_pair)
    joined = jnp.stack(
        [
            0.5 * (conv_real - back_imag + mirror_back[0]),
            0.5 * (conv_imag + back_real - mirror_back[1]),
        ]
    )
    outputs = inverse_series(joined[None])
    conv_out = outputs[0]
    grad_mixed = outputs[1]
    mixer_out = (query_series.astype(jnp.float32) * conv_out).astype(jnp.bfloat16)
    grad_queries = (grad_out.astype(jnp.float32) * conv_out).astype(jnp.bfloat16)
    grad_keys = (grad_mixed * gating * value_series.astype(jnp.float32)).astype(jnp.bfloat16)
    grad_values = (grad_mixed * gating * key_series.astype(jnp.float32)).astype(jnp.bfloat16)
    return (mixer_out, grad_queries, grad_keys, grad_values, grad_spectrum)


SUB = 16
LANES = 128


def split_table(values):
    exact = np.asarray(values, np.float32)
    high = exact.astype(jnp.bfloat16)
    low = (exact - high.astype(np.float32)).astype(jnp.bfloat16)
    return np.stack([high, low], axis=-3)


def device_tables(devices):
    classes = 2 * devices
    turns = 2.0 * np.pi * (np.outer(np.arange(devices), np.arange(devices)) % classes) / classes
    small = np.stack([np.cos(turns), -np.sin(turns)], axis=1)
    small[0, 1] = np.where(np.arange(devices) % 2 == 0, 1.0, -1.0)
    small = small.reshape(classes, devices)
    full = np.kron(small, np.eye(SUB))
    return split_table(full), split_table(full.T)


def row_tables(devices, rows):
    classes = 2 * devices
    length = classes * rows
    half = rows // 2
    place = np.arange(rows)
    tables = np.zeros((devices, 2, rows, 2, rows))
    for group in range(1, devices):
        freq = group + classes * place
        angle = 2.0 * np.pi * (np.outer(freq, place) % length) / length
        tables[group, 0, :, 0] = np.cos(angle)
        tables[group, 0, :, 1] = np.sin(angle)
        tables[group, 1, :, 0] = -np.sin(angle)
        tables[group, 1, :, 1] = np.cos(angle)
    for part, first in ((0, 0), (1, devices)):
        freq = first + classes * np.arange(half)
        angle = 2.0 * np.pi * (np.outer(freq, place) % length) / length
        tables[0, 0, part * half : (part + 1) * half, part] = np.cos(angle)
        tables[0, 1, part * half : (part + 1) * half, part] = -np.sin(angle)
    tables[0, 1, 0, 0] = np.where(place % 2 == 0, 1.0, -1.0)
    tables = tables.reshape(devices, 2 * rows, 2 * rows) / math.sqrt(length)
    return split_table(tables), split_table(tables.transpose(0, 2, 1))


def fold_tables(rows):
    half = rows // 2
    fold = np.zeros((2, 2, rows, 2, 2, rows))
    spread = np.zeros((2, 2, 2, rows, 2, rows))
    for d in range(rows):
        for part, sign in ((0, 1.0), (1, -1.0)):
            fold[1, part, d, part, 0, d] = 1.0
            fold[1, part, d, part, 1, rows - 1 - d] = sign
            spread[1, part, 0, d, part, d] = 1.0
            spread[1, part, 1, rows - 1 - d, part, d] = sign
    for d in range(half):
        for part, sign in ((0, 1.0), (1, -1.0)):
            if d > 0:
                fold[0, part, d, part, 0, d] = 1.0
                fold[0, part, d, part, 0, rows - d] = sign
                spread[0, part, 0, d, part, d] = 1.0
                spread[0, part, 0, rows - d, part, d] = sign
            fold[0, part, half + d, part, 1, d] = 1.0
            fold[0, part, half + d, part, 1, rows - 1 - d] = sign
            spread[0, part, 1, d, part, half + d] = 1.0
            spread[0, part, 1, rows - 1 - d, part, half + d] = sign
    fold[0, 0, 0, 0, 0, 0] = 1.0
    fold[0, 1, 0, 0, 0, half] = 1.0
    spread[0, 0, 0, 0, 0, 0] = 1.0
    spread[0, 0, 0, half, 1, 0] = 1.0
    return (
        fold.reshape(2, 2 * rows, 4 * rows).astype(jnp.bfloat16),
        spread.reshape(2, 4 * rows, 2 * rows).astype(jnp.bfloat16),
    )


def dot(left, right):
    return jnp.dot(left, right, preferred_element_type=jnp.float32)


def gate_column(mask):
    rows = mask.shape[1]
    across = lax.broadcasted_iota(jnp.int32, (rows, rows), 1)
    down = lax.broadcasted_iota(jnp.int32, (rows, rows), 0)
    spots = jnp.where(across == down, mask.astype(jnp.float32), 0.0)
    return jnp.sum(spots, axis=1, keepdims=True)


def exchange_kernel(
    devices,
    groups,
    rows,
    width,
    gate_ref,
    query_hbm,
    key_hbm,
    value_hbm,
    grad_hbm,
    fold_hbm,
    filter_hbm,
    mix_hbm,
    table_hbm,
    back_hbm,
    unmix_hbm,
    spread_hbm,
    got_series,
    spectrum_hbm,
    query_ref,
    key_ref,
    value_ref,
    grad_ref,
    fold_ref,
    filter_ref,
    mix_ref,
    table_ref,
    back_ref,
    unmix_ref,
    spread_ref,
    got_grad,
    send_signal,
    got_signal,
    send_filter,
    got_filter,
    mixed,
    turned,
    send_grad,
    send_series,
    send_sems,
    recv_sems,
    local_sems,
):
    me = lax.axis_index("ctx")
    lane = lax.axis_index("grp")
    barrier = pltpu.get_barrier_semaphore()
    own_fold = jnp.where(me == 0, 0, 1)
    loads = [
        pltpu.make_async_copy(source, target, local_sems.at[2 + at])
        for at, (source, target) in enumerate(
            (
                (query_hbm, query_ref),
                (key_hbm, key_ref),
                (value_hbm, value_ref),
                (grad_hbm, grad_ref),
                (fold_hbm.at[own_fold], fold_ref),
                (filter_hbm, filter_ref),
                (mix_hbm, mix_ref),
                (table_hbm, table_ref),
                (back_hbm, back_ref),
                (unmix_hbm, unmix_ref),
                (spread_hbm.at[own_fold], spread_ref),
            )
        )
    ]
    for load in loads:
        load.start()

    def greet(step, _):
        pl.semaphore_signal(
            barrier,
            inc=1,
            device_id={"ctx": lax.rem(me + step, devices)},
            device_id_type=pl.DeviceIdType.MESH,
        )
        return 0

    lax.fori_loop(1, devices, greet, 0)
    for step in range(1, groups):
        pl.semaphore_signal(
            barrier,
            inc=1,
            device_id={"grp": lax.rem(lane + step, groups)},
            device_id_type=pl.DeviceIdType.MESH,
        )

    near = devices // 2
    side = me // near
    spot = lax.rem(me, near)

    def partner_at(step, direction):
        step = step + step // near
        half_at = lax.rem(side + 1 + step // near, 2)
        return half_at * near + lax.rem(spot + near + direction * lax.rem(step, near), near)

    def remote(kind, source, target, step_from, to):
        return pltpu.make_async_remote_copy(
            src_ref=source.at[to],
            dst_ref=target.at[step_from],
            send_sem=send_sems.at[kind, to],
            recv_sem=recv_sems.at[kind, step_from],
            device_id={"ctx": to},
            device_id_type=pl.DeviceIdType.MESH,
        )

    def relay(step, group):
        return pltpu.make_async_remote_copy(
            src_ref=got_filter.at[group],
            dst_ref=got_filter.at[group],
            send_sem=send_sems.at[3 + step, group],
            recv_sem=recv_sems.at[1, group],
            device_id={"grp": lax.rem(lane + step, groups)},
            device_id_type=pl.DeviceIdType.MESH,
        )

    def start_all(kind, source, target):
        def body(step, _):
            remote(kind, source, target, me, partner_at(step, 1)).start()
            return 0

        lax.fori_loop(0, devices - 1, body, 0)

    def wait_received(kind, source, target):
        def body(step, _):
            other = partner_at(step, -1)
            remote(kind, source, target, other, other).wait_recv()
            return 0

        lax.fori_loop(0, devices - 1, body, 0)

    def wait_sent(kind, source, target):
        def body(step, _):
            remote(kind, source, target, me, partner_at(step, 1)).wait_send()
            return 0

        lax.fori_loop(0, devices - 1, body, 0)

    for load in loads[:4]:
        load.wait()
    gating = gate_column(gate_ref[...])

    def columns_of(block):
        return pl.ds(pl.multiple_of(block * width, width), width)

    def make_signal(to):
        span = columns_of(to)
        gated = gating * key_ref[:, span].astype(jnp.float32) * value_ref[:, span].astype(jnp.float32)
        back = query_ref[:, span].astype(jnp.float32) * grad_ref[:, span].astype(jnp.float32)
        return gated.astype(jnp.bfloat16), back.astype(jnp.bfloat16)

    pl.semaphore_wait(barrier, devices + groups - 2)

    def ship_signal(step, _):
        to = partner_at(step, 1)
        send_signal[to, 0], send_signal[to, 1] = make_signal(to)
        remote(0, send_signal, got_signal, me, to).start()
        return 0

    lax.fori_loop(0, devices - 1, ship_signal, 0)
    got_signal[me, 0], got_signal[me, 1] = make_signal(me)

    for load in loads[4:6]:
        load.wait()
    mine = lax.rem(me, groups) == lane

    @pl.when(mine)
    def _():
        for to in range(devices):
            span = slice(to * width, (to + 1) * width)
            block = filter_ref[:, span]
            high = block.astype(jnp.bfloat16)
            low = (block - high.astype(jnp.float32)).astype(jnp.bfloat16)
            folded = dot(fold_ref[...], high) + dot(fold_ref[...], low)
            send_filter[to] = folded.astype(jnp.bfloat16)
        start_all(1, send_filter, got_filter)
        got_filter[me] = send_filter[me]

    for load in loads[6:]:
        load.wait()
    wait_received(0, send_signal, got_signal)

    def mix(part, _):
        span = pl.ds(pl.multiple_of(part * SUB, SUB), SUB)
        columns = jnp.concatenate(
            [got_signal[:, which, span, :].reshape(devices * SUB, width) for which in (0, 1)], axis=1
        )
        result = dot(mix_ref[0], columns) + dot(mix_ref[1], columns)
        mixed[:, span, :] = result.astype(jnp.bfloat16).reshape(2 * devices, SUB, 2 * width)
        return 0

    lax.fori_loop(0, rows // SUB, mix, 0)

    row_index = lax.broadcasted_iota(jnp.int32, (rows, width), 0)

    def one_group(group):
        source = mixed[pl.ds(2 * group, 2)].reshape(2 * rows, 2 * width)
        spectra = dot(table_ref[group, 0], source) + dot(table_ref[group, 1], source)
        signal_real = spectra[:rows, :width]
        signal_imag = spectra[rows:, :width]
        adjoint_real = spectra[:rows, width:]
        adjoint_imag = spectra[rows:, width:]
        response = got_filter[group].astype(jnp.float32)
        filter_real = response[:rows]
        filter_imag = response[rows:]
        real_pair = jnp.logical_and(row_index == 0, group == 0)

        def times(first_real, first_imag, second_real, second_imag, sign):
            both = first_imag * second_imag
            real = first_real * second_real - jnp.where(real_pair, 0.0, sign * both)
            imag = jnp.where(real_pair, both, first_imag * second_real + sign * first_real * second_imag)
            return real, imag

        grad_real, grad_imag = times(adjoint_real, adjoint_imag, signal_real, signal_imag, -1.0)
        send_grad[group, :rows] = grad_real.astype(jnp.bfloat16)
        send_grad[group, rows:] = grad_imag.astype(jnp.bfloat16)

        @pl.when(group != me)
        def _():
            remote(2, send_grad, got_grad, me, group).start()

        conv_real, conv_imag = times(signal_real, signal_imag, filter_real, filter_imag, 1.0)
        back_real, back_imag = times(adjoint_real, adjoint_imag, filter_real, filter_imag, -1.0)
        product = jnp.concatenate(
            [
                jnp.concatenate([conv_real, back_real], axis=1),
                jnp.concatenate([conv_imag, back_imag], axis=1),
            ],
            axis=0,
        ).astype(jnp.bfloat16)
        result = dot(back_ref[group, 0], product) + dot(back_ref[group, 1], product)
        turned[pl.ds(2 * group, 2)] = result.astype(jnp.bfloat16).reshape(2, rows, 2 * width)

    turns = near // groups

    def in_turn(shift):
        share = lax.rem(lane + shift, groups)

        def body(turn, _):
            half_at = lax.rem(side + 1 + turn // turns, 2)
            place = lax.rem(spot // groups + turns - lax.rem(turn, turns), turns)
            group = half_at * near + place * groups + share

            if shift == 0:

                @pl.when(group != me)
                def _():
                    remote(1, send_filter, got_filter, group, group).wait_recv()

                for step in range(1, groups):
                    relay(step, group).start()
            else:
                relay(shift, group).wait_recv()
            one_group(group)
            return 0

        return body

    for shift in range(groups):
        lax.fori_loop(0, devices // groups, in_turn(shift), 0)
    got_grad[me] = send_grad[me]

    def unmix(part, _):
        span = pl.ds(pl.multiple_of(part * SUB, SUB), SUB)
        columns = turned[:, span, :].reshape(2 * devices * SUB, 2 * width)
        result = dot(unmix_ref[0], columns) + dot(unmix_ref[1], columns)
        result = result.astype(jnp.bfloat16).reshape(devices, SUB, 2 * width)
        send_series[:, 0, span, :] = result[:, :, :width]
        send_series[:, 1, span, :] = result[:, :, width:]
        return 0

    lax.fori_loop(0, rows // SUB, unmix, 0)
    start_all(3, send_series, got_series)
    own_series = pltpu.make_async_copy(send_series.at[me], got_series.at[me], local_sems.at[1])
    own_series.start()

    def spread_block(other):
        filter_ref[:, columns_of(other)] = dot(spread_ref[...], got_grad[other])

    def spread_next(step, _):
        other = partner_at(step, -1)
        remote(2, send_grad, got_grad, other, other).wait_recv()
        spread_block(other)
        return 0

    spread_block(me)
    lax.fori_loop(0, devices - 1, spread_next, 0)
    spectrum_copy = pltpu.make_async_copy(filter_ref, spectrum_hbm, local_sems.at[0])
    spectrum_copy.start()
    own_series.wait()
    wait_received(3, send_series, got_series)
    wait_sent(0, send_signal, got_signal)

    @pl.when(mine)
    def _():
        wait_sent(1, send_filter, got_filter)

    def relays_sent(turn, _):
        for step in range(1, groups):
            relay(step, turn * groups + lane).wait_send()
        return 0

    lax.fori_loop(0, devices // groups, relays_sent, 0)
    wait_sent(2, send_grad, got_grad)
    wait_sent(3, send_series, got_series)
    spectrum_copy.wait()


def finish_kernel(
    blocks,
    width,
    query_ref,
    key_ref,
    value_ref,
    grad_ref,
    gate_ref,
    series_ref,
    mixer_out,
    queries_out,
    keys_out,
    values_out,
):
    gating = gate_column(gate_ref[...])
    for block in range(blocks):
        span = slice(block * width, (block + 1) * width)
        conv = series_ref[block, 0].astype(jnp.float32)
        back = series_ref[block, 1].astype(jnp.float32) * gating
        mixer_out[:, span] = (query_ref[:, span].astype(jnp.float32) * conv).astype(jnp.bfloat16)
        queries_out[:, span] = (grad_ref[:, span].astype(jnp.float32) * conv).astype(jnp.bfloat16)
        keys_out[:, span] = (back * value_ref[:, span].astype(jnp.float32)).astype(jnp.bfloat16)
        values_out[:, span] = (back * key_ref[:, span].astype(jnp.float32)).astype(jnp.bfloat16)


def wide_shards(query_series, key_series, value_series, grad_out, gate_mask, filter_spectrum):
    devices = lax.axis_size("ctx")
    rows, channels = query_series.shape
    width = channels // devices
    gating = gate_mask[None, :]
    mix_table, unmix_table = device_tables(devices)
    forward_table, back_table = row_tables(devices, rows)
    folds, spreads = fold_tables(rows)
    groups = lax.axis_size("grp")
    half = jnp.bfloat16
    vmem = pl.BlockSpec(memory_space=pltpu.VMEM)
    anywhere = pl.BlockSpec(memory_space=pl.ANY)
    spectrum_block = (devices, 2 * rows, width)
    series_block = (devices, 2, rows, width)
    got_series, spectrum = pl.pallas_call(
        functools.partial(exchange_kernel, devices, groups, rows, width),
        out_shape=(
            jax.ShapeDtypeStruct(series_block, half),
            jax.ShapeDtypeStruct((4 * rows, channels), jnp.float32),
        ),
        in_specs=[vmem] + [anywhere] * 11,
        out_specs=(anywhere, anywhere),
        scratch_shapes=[pltpu.VMEM((rows, channels), half)] * 4
        + [
            pltpu.VMEM((2 * rows, 4 * rows), half),
            pltpu.VMEM((4 * rows, channels), jnp.float32),
            pltpu.VMEM(mix_table.shape, half),
            pltpu.VMEM(forward_table.shape, half),
            pltpu.VMEM(back_table.shape, half),
            pltpu.VMEM(unmix_table.shape, half),
            pltpu.VMEM((4 * rows, 2 * rows), half),
            pltpu.VMEM(spectrum_block, half),
            pltpu.VMEM(series_block, half),
            pltpu.VMEM(series_block, half),
            pltpu.VMEM(spectrum_block, half),
            pltpu.VMEM(spectrum_block, half),
            pltpu.VMEM((2 * devices, rows, 2 * width), half),
            pltpu.VMEM((2 * devices, rows, 2 * width), half),
            pltpu.VMEM(spectrum_block, half),
            pltpu.VMEM(series_block, half),
            pltpu.SemaphoreType.DMA((3 + groups, devices)),
            pltpu.SemaphoreType.DMA((4, devices)),
            pltpu.SemaphoreType.DMA((13,)),
        ],
        compiler_params=pltpu.CompilerParams(
            collective_id=0, has_side_effects=True, vmem_limit_bytes=60 * 1024 * 1024
        ),
        name="exchange",
    )(
        gating,
        query_series,
        key_series,
        value_series,
        grad_out,
        jnp.asarray(folds),
        filter_spectrum.reshape(4 * rows, channels),
        jnp.asarray(mix_table),
        jnp.asarray(forward_table),
        jnp.asarray(back_table),
        jnp.asarray(unmix_table),
        jnp.asarray(spreads),
    )
    blocks = math.gcd(devices, 4)
    columns = pl.BlockSpec((rows, blocks * width), lambda step: (0, step))
    mixer_out, queries, keys, values = pl.pallas_call(
        functools.partial(finish_kernel, blocks, width),
        grid=(devices // blocks,),
        out_shape=(jax.ShapeDtypeStruct((rows, channels), half),) * 4,
        in_specs=[
            columns,
            columns,
            columns,
            columns,
            pl.BlockSpec((1, rows), lambda step: (0, 0)),
            pl.BlockSpec((blocks, 2, rows, width), lambda step: (step, 0, 0, 0)),
        ],
        out_specs=(columns,) * 4,
        compiler_params=pltpu.CompilerParams(vmem_limit_bytes=32 * 1024 * 1024),
        name="finish",
    )(query_series, key_series, value_series, grad_out, gating, got_series)
    return mixer_out, queries, keys, values, spectrum.reshape(2, 2, rows, channels)


def shards(query_series, *others):
    devices = lax.axis_size("ctx")
    rows, channels = query_series.shape
    if rows % SUB == 0 and channels % (devices * LANES) == 0 and devices % (2 * lax.axis_size("grp")) == 0:
        return wide_shards(query_series, *others)
    return narrow_shards(query_series, *others)


def solution(mesh):
    placed = (
        P(("grp", "ctx"), None),
        P(("grp", "ctx"), None),
        P(("grp", "ctx"), None),
        P(("grp", "ctx"), None),
        P(("grp", "ctx")),
        P(None, "ctx", None, None),
    )
    return jax.shard_map(
        shards,
        mesh=mesh,
        in_specs=placed,
        out_specs=(
            P(("grp", "ctx"), None),
            P(("grp", "ctx"), None),
            P(("grp", "ctx"), None),
            P(("grp", "ctx"), None),
            P(None, ("grp", "ctx"), None, None),
        ),
        check_vma=False,
    )
```

```python
import functools
import math

import jax
import jax.numpy as jnp
import numpy as np
from jax import lax
from jax.experimental import pallas as pl
from jax.experimental.pallas import tpu as pltpu
from jax.sharding import PartitionSpec as P

highest = lax.Precision.HIGHEST


def class_order(devices):
    indices = np.arange(2 * devices)
    pair_index = indices // 2
    parity = indices % 2
    return np.where(
        pair_index == 0,
        parity * devices,
        np.where(parity == 0, pair_index, 2 * devices - pair_index),
    )


def partner(spectrum):
    flipped = jnp.flip(spectrum, axis=-2)
    crossed = jnp.flip(flipped, axis=-3)
    anchor_head = jnp.roll(flipped[..., 0:1, :, :], 1, axis=-2)
    anchor = jnp.concatenate([anchor_head, flipped[..., 1:2, :, :]], axis=-3)
    return jnp.where(lax.axis_index("ctx") == 0, anchor, crossed)


def forward_spectra(series):
    devices = lax.axis_size("ctx")
    tok_rows = series.shape[1]
    group_rows = tok_rows // devices
    classes = 2 * devices
    fft_length = classes * tok_rows
    ordering = class_order(devices)
    norm_factor = 1.0 / math.sqrt(fft_length)
    positions = lax.axis_index("ctx") * group_rows + jnp.arange(group_rows, dtype=jnp.int32)
    offsets = jnp.arange(devices, dtype=jnp.int32) * tok_rows
    order_column = jnp.asarray(ordering, jnp.int32)[:, None, None]
    first_turns = order_column * (offsets[None, :, None] + positions[None, None, :]) % fft_length
    first_angle = first_turns.astype(jnp.float32) * (-2.0 * math.pi / fft_length)
    first_table = jnp.stack([jnp.cos(first_angle), jnp.sin(first_angle)])
    rows_index = np.arange(tok_rows)
    second_angle = 2.0 * np.pi * (np.outer(rows_index, rows_index) % tok_rows) / tok_rows
    cos_second = np.cos(second_angle)
    sin_second = -np.sin(second_angle)
    row_real = np.stack([cos_second, -sin_second], axis=1)
    row_imag = np.stack([sin_second, cos_second], axis=1)
    second_table = jnp.asarray(np.stack([row_real, row_imag]) * norm_factor, jnp.float32)
    shaped = series.reshape(2, devices, group_rows, series.shape[-1])
    received = lax.all_to_all(shaped, "ctx", split_axis=1, concat_axis=1, tiled=True)
    channels = received.shape[-1]
    widened = received.astype(jnp.float32)
    parts = jnp.einsum("qjab,sabx->sqjbx", first_table, widened, precision=highest)
    parts = jnp.stack([parts[0, 0] - parts[1, 1], parts[0, 1] + parts[1, 0]])[None]
    signals = parts.shape[0]
    stacked = parts.reshape(signals * 2, devices, 2, group_rows, channels)
    received = lax.all_to_all(stacked, "ctx", split_axis=1, concat_axis=3, tiled=True)
    channels = received.shape[-1]
    signals = received.shape[0] // 2
    shaped = received.reshape(signals, 2, 2, tok_rows, channels)
    joined = jnp.einsum("qdpb,speby->sqedy", second_table, shaped, precision=highest)
    spectrum = joined.reshape(signals * 2, 2, tok_rows, channels)
    return spectrum.reshape(spectrum.shape[0] // 2, 2, 2, tok_rows, series.shape[-1])


def inverse_series(spectra):
    devices = lax.axis_size("ctx")
    signals = spectra.shape[0]
    tok_rows = spectra.shape[3]
    channels_all = spectra.shape[4]
    group_rows = tok_rows // devices
    classes = 2 * devices
    fft_length = classes * tok_rows
    ordering = class_order(devices)
    norm_factor = 1.0 / math.sqrt(fft_length)
    location = lax.axis_index("ctx")
    own_classes = jnp.stack(
        [
            jnp.where(location == 0, 0, location),
            jnp.where(location == 0, devices, classes - location),
        ]
    )
    rows_index = jnp.arange(tok_rows, dtype=jnp.int32)
    square_turns = rows_index[:, None] * rows_index[None, :] * classes % fft_length
    second_turns = (
        square_turns[None, :, :] + own_classes[:, None, None] * rows_index[None, :, None]
    ) % fft_length
    second_angle = second_turns.astype(jnp.float32) * (2.0 * math.pi / fft_length)
    cos_second = jnp.cos(second_angle)
    sin_second = jnp.sin(second_angle)
    second_table = jnp.stack(
        [jnp.stack([cos_second, -sin_second], axis=2), jnp.stack([sin_second, cos_second], axis=2)],
        axis=1,
    )
    stacked = jnp.einsum("eqbpd,spedy->sqeby", second_table, spectra, precision=highest)
    stacked = stacked.reshape(signals * 2, 1, 2, tok_rows, channels_all)
    first_angle = 2.0 * np.pi * (np.outer(np.arange(devices), ordering) % classes) / classes
    cos_first = np.cos(first_angle)
    sin_first = np.sin(first_angle)
    full_table = (
        np.stack(
            [np.stack([cos_first, -sin_first], axis=1), np.stack([sin_first, cos_first], axis=1)]
        )
        * norm_factor
    )
    first_table = jnp.asarray(full_table, jnp.float32)
    received = lax.all_to_all(stacked, "ctx", split_axis=3, concat_axis=1, tiled=True)
    channels = received.shape[-1]
    flattened = received.reshape(signals, 2, classes, group_rows * channels)
    time_series = jnp.einsum("qapj,spjx->sqax", first_table, flattened, precision=highest)
    time_series = time_series.reshape(2, devices, group_rows, channels)
    outputs = lax.all_to_all(time_series, "ctx", split_axis=1, concat_axis=1, tiled=True)
    return outputs.reshape(2, tok_rows, channels_all)


def narrow_shards(query_series, key_series, value_series, grad_out, gate_mask, filter_spectrum):
    gating = gate_mask.astype(jnp.float32)[:, None]
    gated_pair = (
        gating * key_series.astype(jnp.float32) * value_series.astype(jnp.float32)
    ).astype(jnp.bfloat16)
    back_signal = (query_series.astype(jnp.float32) * grad_out.astype(jnp.float32)).astype(
        jnp.bfloat16
    )
    series = jnp.stack([gated_pair, back_signal])
    filter_real = filter_spectrum[0]
    filter_imag = filter_spectrum[1]
    combined = forward_spectra(series)[0]
    mirror = partner(combined)
    signal_real = 0.5 * (combined[0] + mirror[0])
    signal_imag = 0.5 * (combined[1] - mirror[1])
    adjoint_real = 0.5 * (combined[1] + mirror[1])
    adjoint_imag = 0.5 * (mirror[0] - combined[0])
    conv_real = signal_real * filter_real - signal_imag * filter_imag
    conv_imag = signal_real * filter_imag + signal_imag * filter_real
    back_real = adjoint_real * filter_real + adjoint_imag * filter_imag
    back_imag = adjoint_imag * filter_real - adjoint_real * filter_imag
    grad_spectrum = jnp.stack(
        [
            adjoint_real * signal_real + adjoint_imag * signal_imag,
            adjoint_imag * signal_real - adjoint_real * signal_imag,
        ]
    )
    minus_pair = jnp.stack([conv_real + back_imag, conv_imag - back_real])
    mirror_back = partner(minus_pair)
    joined = jnp.stack(
        [
            0.5 * (conv_real - back_imag + mirror_back[0]),
            0.5 * (conv_imag + back_real - mirror_back[1]),
        ]
    )
    outputs = inverse_series(joined[None])
    conv_out = outputs[0]
    grad_mixed = outputs[1]
    mixer_out = (query_series.astype(jnp.float32) * conv_out).astype(jnp.bfloat16)
    grad_queries = (grad_out.astype(jnp.float32) * conv_out).astype(jnp.bfloat16)
    grad_keys = (grad_mixed * gating * value_series.astype(jnp.float32)).astype(jnp.bfloat16)
    grad_values = (grad_mixed * gating * key_series.astype(jnp.float32)).astype(jnp.bfloat16)
    return (mixer_out, grad_queries, grad_keys, grad_values, grad_spectrum)


SUB = 16
LANES = 128


def split_table(values):
    exact = np.asarray(values, np.float32)
    high = exact.astype(jnp.bfloat16)
    low = (exact - high.astype(np.float32)).astype(jnp.bfloat16)
    return np.stack([high, low], axis=-3)


def device_tables(devices):
    classes = 2 * devices
    turns = 2.0 * np.pi * (np.outer(np.arange(devices), np.arange(devices)) % classes) / classes
    small = np.stack([np.cos(turns), -np.sin(turns)], axis=1)
    small[0, 1] = np.where(np.arange(devices) % 2 == 0, 1.0, -1.0)
    small = small.reshape(classes, devices)
    full = np.kron(small, np.eye(SUB))
    return split_table(full), split_table(full.T)


def row_tables(devices, rows):
    classes = 2 * devices
    length = classes * rows
    half = rows // 2
    place = np.arange(rows)
    tables = np.zeros((devices, 2, rows, 2, rows))
    for group in range(1, devices):
        freq = group + classes * place
        angle = 2.0 * np.pi * (np.outer(freq, place) % length) / length
        tables[group, 0, :, 0] = np.cos(angle)
        tables[group, 0, :, 1] = np.sin(angle)
        tables[group, 1, :, 0] = -np.sin(angle)
        tables[group, 1, :, 1] = np.cos(angle)
    for part, first in ((0, 0), (1, devices)):
        freq = first + classes * np.arange(half)
        angle = 2.0 * np.pi * (np.outer(freq, place) % length) / length
        tables[0, 0, part * half : (part + 1) * half, part] = np.cos(angle)
        tables[0, 1, part * half : (part + 1) * half, part] = -np.sin(angle)
    tables[0, 1, 0, 0] = np.where(place % 2 == 0, 1.0, -1.0)
    tables = tables.reshape(devices, 2 * rows, 2 * rows) / math.sqrt(length)
    return split_table(tables), split_table(tables.transpose(0, 2, 1))


def fold_tables(rows):
    half = rows // 2
    fold = np.zeros((2, 2, rows, 2, 2, rows))
    spread = np.zeros((2, 2, 2, rows, 2, rows))
    for d in range(rows):
        for part, sign in ((0, 1.0), (1, -1.0)):
            fold[1, part, d, part, 0, d] = 1.0
            fold[1, part, d, part, 1, rows - 1 - d] = sign
            spread[1, part, 0, d, part, d] = 1.0
            spread[1, part, 1, rows - 1 - d, part, d] = sign
    for d in range(half):
        for part, sign in ((0, 1.0), (1, -1.0)):
            if d > 0:
                fold[0, part, d, part, 0, d] = 1.0
                fold[0, part, d, part, 0, rows - d] = sign
                spread[0, part, 0, d, part, d] = 1.0
                spread[0, part, 0, rows - d, part, d] = sign
            fold[0, part, half + d, part, 1, d] = 1.0
            fold[0, part, half + d, part, 1, rows - 1 - d] = sign
            spread[0, part, 1, d, part, half + d] = 1.0
            spread[0, part, 1, rows - 1 - d, part, half + d] = sign
    fold[0, 0, 0, 0, 0, 0] = 1.0
    fold[0, 1, 0, 0, 0, half] = 1.0
    spread[0, 0, 0, 0, 0, 0] = 1.0
    spread[0, 0, 0, half, 1, 0] = 1.0
    return (
        fold.reshape(2, 2 * rows, 4 * rows).astype(jnp.bfloat16),
        spread.reshape(2, 4 * rows, 2 * rows).astype(jnp.bfloat16),
    )


def dot(left, right):
    return jnp.dot(left, right, preferred_element_type=jnp.float32)


def gate_column(mask):
    rows = mask.shape[1]
    across = lax.broadcasted_iota(jnp.int32, (rows, rows), 1)
    down = lax.broadcasted_iota(jnp.int32, (rows, rows), 0)
    spots = jnp.where(across == down, mask.astype(jnp.float32), 0.0)
    return jnp.sum(spots, axis=1, keepdims=True)


def exchange_kernel(
    devices,
    groups,
    rows,
    width,
    gate_ref,
    query_hbm,
    key_hbm,
    value_hbm,
    grad_hbm,
    fold_hbm,
    filter_hbm,
    mix_hbm,
    table_hbm,
    back_hbm,
    unmix_hbm,
    got_grad,
    got_series,
    query_ref,
    key_ref,
    value_ref,
    grad_ref,
    fold_ref,
    filter_ref,
    mix_ref,
    table_ref,
    back_ref,
    unmix_ref,
    send_signal,
    got_signal,
    send_filter,
    got_filter,
    mixed,
    turned,
    send_grad,
    send_series,
    send_sems,
    recv_sems,
    local_sems,
):
    me = lax.axis_index("ctx")
    lane = lax.axis_index("grp")
    barrier = pltpu.get_barrier_semaphore()
    own_fold = jnp.where(me == 0, 0, 1)
    loads = [
        pltpu.make_async_copy(source, target, local_sems.at[2 + at])
        for at, (source, target) in enumerate(
            (
                (query_hbm, query_ref),
                (key_hbm, key_ref),
                (value_hbm, value_ref),
                (grad_hbm, grad_ref),
                (fold_hbm.at[own_fold], fold_ref),
                (filter_hbm, filter_ref),
                (mix_hbm, mix_ref),
                (table_hbm, table_ref),
                (back_hbm, back_ref),
                (unmix_hbm, unmix_ref),
            )
        )
    ]
    for load in loads:
        load.start()

    def greet(step, _):
        pl.semaphore_signal(
            barrier,
            inc=1,
            device_id={"ctx": lax.rem(me + step, devices)},
            device_id_type=pl.DeviceIdType.MESH,
        )
        return 0

    lax.fori_loop(1, devices, greet, 0)
    for step in range(1, groups):
        pl.semaphore_signal(
            barrier,
            inc=1,
            device_id={"grp": lax.rem(lane + step, groups)},
            device_id_type=pl.DeviceIdType.MESH,
        )

    near = devices // 2
    side = me // near
    spot = lax.rem(me, near)

    def partner_at(step, direction):
        step = step + step // near
        half_at = lax.rem(side + 1 + step // near, 2)
        return half_at * near + lax.rem(spot + near + direction * lax.rem(step, near), near)

    def remote(kind, source, target, step_from, to):
        return pltpu.make_async_remote_copy(
            src_ref=source.at[to],
            dst_ref=target.at[step_from],
            send_sem=send_sems.at[kind, to],
            recv_sem=recv_sems.at[kind, step_from],
            device_id={"ctx": to},
            device_id_type=pl.DeviceIdType.MESH,
        )

    def relay(step, group):
        return pltpu.make_async_remote_copy(
            src_ref=got_filter.at[group],
            dst_ref=got_filter.at[group],
            send_sem=send_sems.at[3 + step, group],
            recv_sem=recv_sems.at[1, group],
            device_id={"grp": lax.rem(lane + step, groups)},
            device_id_type=pl.DeviceIdType.MESH,
        )

    def start_all(kind, source, target):
        def body(step, _):
            remote(kind, source, target, me, partner_at(step, 1)).start()
            return 0

        lax.fori_loop(0, devices - 1, body, 0)

    def wait_received(kind, source, target):
        def body(step, _):
            other = partner_at(step, -1)
            remote(kind, source, target, other, other).wait_recv()
            return 0

        lax.fori_loop(0, devices - 1, body, 0)

    def wait_sent(kind, source, target):
        def body(step, _):
            remote(kind, source, target, me, partner_at(step, 1)).wait_send()
            return 0

        lax.fori_loop(0, devices - 1, body, 0)

    for load in loads[:4]:
        load.wait()
    gating = gate_column(gate_ref[...])

    def make_signal(to):
        span = pl.ds(pl.multiple_of(to * width, width), width)
        gated = gating * key_ref[:, span].astype(jnp.float32) * value_ref[:, span].astype(jnp.float32)
        back = query_ref[:, span].astype(jnp.float32) * grad_ref[:, span].astype(jnp.float32)
        return gated.astype(jnp.bfloat16), back.astype(jnp.bfloat16)

    pl.semaphore_wait(barrier, devices + groups - 2)

    def ship_signal(step, _):
        to = partner_at(step, 1)
        send_signal[to, 0], send_signal[to, 1] = make_signal(to)
        remote(0, send_signal, got_signal, me, to).start()
        return 0

    lax.fori_loop(0, devices - 1, ship_signal, 0)
    got_signal[me, 0], got_signal[me, 1] = make_signal(me)

    for load in loads[4:6]:
        load.wait()
    mine = lax.rem(me, groups) == lane

    @pl.when(mine)
    def _():
        for to in range(devices):
            span = slice(to * width, (to + 1) * width)
            block = filter_ref[:, span]
            high = block.astype(jnp.bfloat16)
            low = (block - high.astype(jnp.float32)).astype(jnp.bfloat16)
            folded = dot(fold_ref[...], high) + dot(fold_ref[...], low)
            send_filter[to] = folded.astype(jnp.bfloat16)
        start_all(1, send_filter, got_filter)
        got_filter[me] = send_filter[me]

    for load in loads[6:]:
        load.wait()
    wait_received(0, send_signal, got_signal)

    def mix(part, _):
        span = pl.ds(pl.multiple_of(part * SUB, SUB), SUB)
        columns = jnp.concatenate(
            [got_signal[:, which, span, :].reshape(devices * SUB, width) for which in (0, 1)], axis=1
        )
        result = dot(mix_ref[0], columns) + dot(mix_ref[1], columns)
        mixed[:, span, :] = result.astype(jnp.bfloat16).reshape(2 * devices, SUB, 2 * width)
        return 0

    lax.fori_loop(0, rows // SUB, mix, 0)

    row_index = lax.broadcasted_iota(jnp.int32, (rows, width), 0)

    def one_group(group):
        source = mixed[pl.ds(2 * group, 2)].reshape(2 * rows, 2 * width)
        spectra = dot(table_ref[group, 0], source) + dot(table_ref[group, 1], source)
        signal_real = spectra[:rows, :width]
        signal_imag = spectra[rows:, :width]
        adjoint_real = spectra[:rows, width:]
        adjoint_imag = spectra[rows:, width:]
        response = got_filter[group].astype(jnp.float32)
        filter_real = response[:rows]
        filter_imag = response[rows:]
        real_pair = jnp.logical_and(row_index == 0, group == 0)

        def times(first_real, first_imag, second_real, second_imag, sign):
            both = first_imag * second_imag
            real = first_real * second_real - jnp.where(real_pair, 0.0, sign * both)
            imag = jnp.where(real_pair, both, first_imag * second_real + sign * first_real * second_imag)
            return real, imag

        grad_real, grad_imag = times(adjoint_real, adjoint_imag, signal_real, signal_imag, -1.0)
        send_grad[group, :rows] = grad_real.astype(jnp.bfloat16)
        send_grad[group, rows:] = grad_imag.astype(jnp.bfloat16)

        @pl.when(group != me)
        def _():
            remote(2, send_grad, got_grad, me, group).start()

        conv_real, conv_imag = times(signal_real, signal_imag, filter_real, filter_imag, 1.0)
        back_real, back_imag = times(adjoint_real, adjoint_imag, filter_real, filter_imag, -1.0)
        product = jnp.concatenate(
            [
                jnp.concatenate([conv_real, back_real], axis=1),
                jnp.concatenate([conv_imag, back_imag], axis=1),
            ],
            axis=0,
        ).astype(jnp.bfloat16)
        result = dot(back_ref[group, 0], product) + dot(back_ref[group, 1], product)
        turned[pl.ds(2 * group, 2)] = result.astype(jnp.bfloat16).reshape(2, rows, 2 * width)

    turns = near // groups

    def in_turn(shift):
        share = lax.rem(lane + shift, groups)

        def body(turn, _):
            half_at = lax.rem(side + 1 + turn // turns, 2)
            place = lax.rem(spot // groups + turns - lax.rem(turn, turns), turns)
            group = half_at * near + place * groups + share

            if shift == 0:

                @pl.when(group != me)
                def _():
                    remote(1, send_filter, got_filter, group, group).wait_recv()

                for step in range(1, groups):
                    relay(step, group).start()
            else:
                relay(shift, group).wait_recv()
            one_group(group)
            return 0

        return body

    for shift in range(groups):
        lax.fori_loop(0, devices // groups, in_turn(shift), 0)
    own_grad = pltpu.make_async_copy(send_grad.at[me], got_grad.at[me], local_sems.at[0])
    own_grad.start()

    def unmix(part, _):
        span = pl.ds(pl.multiple_of(part * SUB, SUB), SUB)
        columns = turned[:, span, :].reshape(2 * devices * SUB, 2 * width)
        result = dot(unmix_ref[0], columns) + dot(unmix_ref[1], columns)
        result = result.astype(jnp.bfloat16).reshape(devices, SUB, 2 * width)
        send_series[:, 0, span, :] = result[:, :, :width]
        send_series[:, 1, span, :] = result[:, :, width:]
        return 0

    lax.fori_loop(0, rows // SUB, unmix, 0)
    start_all(3, send_series, got_series)
    own_series = pltpu.make_async_copy(send_series.at[me], got_series.at[me], local_sems.at[1])
    own_series.start()
    own_grad.wait()
    own_series.wait()
    wait_received(2, send_grad, got_grad)
    wait_received(3, send_series, got_series)
    wait_sent(0, send_signal, got_signal)

    @pl.when(mine)
    def _():
        wait_sent(1, send_filter, got_filter)

    def relays_sent(turn, _):
        for step in range(1, groups):
            relay(step, turn * groups + lane).wait_send()
        return 0

    lax.fori_loop(0, devices // groups, relays_sent, 0)
    wait_sent(2, send_grad, got_grad)
    wait_sent(3, send_series, got_series)


def finish_kernel(
    blocks,
    width,
    query_ref,
    key_ref,
    value_ref,
    grad_ref,
    gate_ref,
    spread_ref,
    half_ref,
    series_ref,
    mixer_out,
    queries_out,
    keys_out,
    values_out,
    spectrum_out,
):
    gating = gate_column(gate_ref[...])
    own_spread = jnp.where(lax.axis_index("ctx") == 0, 0, 1)
    for block in range(blocks):
        span = slice(block * width, (block + 1) * width)
        conv = series_ref[block, 0].astype(jnp.float32)
        back = series_ref[block, 1].astype(jnp.float32) * gating
        mixer_out[:, span] = (query_ref[:, span].astype(jnp.float32) * conv).astype(jnp.bfloat16)
        queries_out[:, span] = (grad_ref[:, span].astype(jnp.float32) * conv).astype(jnp.bfloat16)
        keys_out[:, span] = (back * value_ref[:, span].astype(jnp.float32)).astype(jnp.bfloat16)
        values_out[:, span] = (back * key_ref[:, span].astype(jnp.float32)).astype(jnp.bfloat16)

    for first in range(0, blocks, 2):
        halves = jnp.concatenate([half_ref[block] for block in range(first, min(first + 2, blocks))], axis=1)
        spectrum_out[:, first * width : first * width + halves.shape[1]] = dot(spread_ref[own_spread], halves)


def wide_shards(query_series, key_series, value_series, grad_out, gate_mask, filter_spectrum):
    devices = lax.axis_size("ctx")
    rows, channels = query_series.shape
    width = channels // devices
    gating = gate_mask[None, :]
    mix_table, unmix_table = device_tables(devices)
    forward_table, back_table = row_tables(devices, rows)
    folds, spreads = fold_tables(rows)
    groups = lax.axis_size("grp")
    half = jnp.bfloat16
    vmem = pl.BlockSpec(memory_space=pltpu.VMEM)
    anywhere = pl.BlockSpec(memory_space=pl.ANY)
    spectrum_block = (devices, 2 * rows, width)
    series_block = (devices, 2, rows, width)
    got_grad, got_series = pl.pallas_call(
        functools.partial(exchange_kernel, devices, groups, rows, width),
        out_shape=(
            jax.ShapeDtypeStruct(spectrum_block, half),
            jax.ShapeDtypeStruct(series_block, half),
        ),
        in_specs=[vmem] + [anywhere] * 10,
        out_specs=(anywhere, anywhere),
        scratch_shapes=[pltpu.VMEM((rows, channels), half)] * 4
        + [
            pltpu.VMEM((2 * rows, 4 * rows), half),
            pltpu.VMEM((4 * rows, channels), jnp.float32),
            pltpu.VMEM(mix_table.shape, half),
            pltpu.VMEM(forward_table.shape, half),
            pltpu.VMEM(back_table.shape, half),
            pltpu.VMEM(unmix_table.shape, half),
            pltpu.VMEM(series_block, half),
            pltpu.VMEM(series_block, half),
            pltpu.VMEM(spectrum_block, half),
            pltpu.VMEM(spectrum_block, half),
            pltpu.VMEM((2 * devices, rows, 2 * width), half),
            pltpu.VMEM((2 * devices, rows, 2 * width), half),
            pltpu.VMEM(spectrum_block, half),
            pltpu.VMEM(series_block, half),
            pltpu.SemaphoreType.DMA((3 + groups, devices)),
            pltpu.SemaphoreType.DMA((4, devices)),
            pltpu.SemaphoreType.DMA((12,)),
        ],
        compiler_params=pltpu.CompilerParams(
            collective_id=0, has_side_effects=True, vmem_limit_bytes=60 * 1024 * 1024
        ),
        name="exchange",
    )(
        gating,
        query_series,
        key_series,
        value_series,
        grad_out,
        jnp.asarray(folds),
        filter_spectrum.reshape(4 * rows, channels),
        jnp.asarray(mix_table),
        jnp.asarray(forward_table),
        jnp.asarray(back_table),
        jnp.asarray(unmix_table),
    )
    blocks = math.gcd(devices, 4)
    columns = pl.BlockSpec((rows, blocks * width), lambda step: (0, step))
    mixer_out, queries, keys, values, spectrum = pl.pallas_call(
        functools.partial(finish_kernel, blocks, width),
        grid=(devices // blocks,),
        out_shape=(jax.ShapeDtypeStruct((rows, channels), half),) * 4
        + (jax.ShapeDtypeStruct((4 * rows, channels), jnp.float32),),
        in_specs=[
            columns,
            columns,
            columns,
            columns,
            pl.BlockSpec((1, rows), lambda step: (0, 0)),
            pl.BlockSpec((2, 4 * rows, 2 * rows), lambda step: (0, 0, 0)),
            pl.BlockSpec((blocks, 2 * rows, width), lambda step: (step, 0, 0)),
            pl.BlockSpec((blocks, 2, rows, width), lambda step: (step, 0, 0, 0)),
        ],
        out_specs=(columns,) * 4 + (pl.BlockSpec((4 * rows, blocks * width), lambda step: (0, step)),),
        compiler_params=pltpu.CompilerParams(vmem_limit_bytes=32 * 1024 * 1024),
        name="finish",
    )(query_series, key_series, value_series, grad_out, gating, jnp.asarray(spreads), got_grad, got_series)
    return mixer_out, queries, keys, values, spectrum.reshape(2, 2, rows, channels)


def shards(query_series, *others):
    devices = lax.axis_size("ctx")
    rows, channels = query_series.shape
    if rows % SUB == 0 and channels % (devices * LANES) == 0 and devices % (2 * lax.axis_size("grp")) == 0:
        return wide_shards(query_series, *others)
    return narrow_shards(query_series, *others)


def solution(mesh):
    placed = (
        P(("grp", "ctx"), None),
        P(("grp", "ctx"), None),
        P(("grp", "ctx"), None),
        P(("grp", "ctx"), None),
        P(("grp", "ctx")),
        P(None, "ctx", None, None),
    )
    return jax.shard_map(
        shards,
        mesh=mesh,
        in_specs=placed,
        out_specs=(
            P(("grp", "ctx"), None),
            P(("grp", "ctx"), None),
            P(("grp", "ctx"), None),
            P(("grp", "ctx"), None),
            P(None, ("grp", "ctx"), None, None),
        ),
        check_vma=False,
    )
```

```python
import functools
import math

import jax
import jax.numpy as jnp
import numpy as np
from jax import lax
from jax.experimental import pallas as pl
from jax.experimental.pallas import tpu as pltpu
from jax.sharding import PartitionSpec as P

highest = lax.Precision.HIGHEST


def class_order(devices):
    indices = np.arange(2 * devices)
    pair_index = indices // 2
    parity = indices % 2
    return np.where(
        pair_index == 0,
        parity * devices,
        np.where(parity == 0, pair_index, 2 * devices - pair_index),
    )


def partner(spectrum):
    flipped = jnp.flip(spectrum, axis=-2)
    crossed = jnp.flip(flipped, axis=-3)
    anchor_head = jnp.roll(flipped[..., 0:1, :, :], 1, axis=-2)
    anchor = jnp.concatenate([anchor_head, flipped[..., 1:2, :, :]], axis=-3)
    return jnp.where(lax.axis_index("ctx") == 0, anchor, crossed)


def forward_spectra(series):
    devices = lax.axis_size("ctx")
    tok_rows = series.shape[1]
    group_rows = tok_rows // devices
    classes = 2 * devices
    fft_length = classes * tok_rows
    ordering = class_order(devices)
    norm_factor = 1.0 / math.sqrt(fft_length)
    positions = lax.axis_index("ctx") * group_rows + jnp.arange(group_rows, dtype=jnp.int32)
    offsets = jnp.arange(devices, dtype=jnp.int32) * tok_rows
    order_column = jnp.asarray(ordering, jnp.int32)[:, None, None]
    first_turns = order_column * (offsets[None, :, None] + positions[None, None, :]) % fft_length
    first_angle = first_turns.astype(jnp.float32) * (-2.0 * math.pi / fft_length)
    first_table = jnp.stack([jnp.cos(first_angle), jnp.sin(first_angle)])
    rows_index = np.arange(tok_rows)
    second_angle = 2.0 * np.pi * (np.outer(rows_index, rows_index) % tok_rows) / tok_rows
    cos_second = np.cos(second_angle)
    sin_second = -np.sin(second_angle)
    row_real = np.stack([cos_second, -sin_second], axis=1)
    row_imag = np.stack([sin_second, cos_second], axis=1)
    second_table = jnp.asarray(np.stack([row_real, row_imag]) * norm_factor, jnp.float32)
    shaped = series.reshape(2, devices, group_rows, series.shape[-1])
    received = lax.all_to_all(shaped, "ctx", split_axis=1, concat_axis=1, tiled=True)
    channels = received.shape[-1]
    widened = received.astype(jnp.float32)
    parts = jnp.einsum("qjab,sabx->sqjbx", first_table, widened, precision=highest)
    parts = jnp.stack([parts[0, 0] - parts[1, 1], parts[0, 1] + parts[1, 0]])[None]
    signals = parts.shape[0]
    stacked = parts.reshape(signals * 2, devices, 2, group_rows, channels)
    received = lax.all_to_all(stacked, "ctx", split_axis=1, concat_axis=3, tiled=True)
    channels = received.shape[-1]
    signals = received.shape[0] // 2
    shaped = received.reshape(signals, 2, 2, tok_rows, channels)
    joined = jnp.einsum("qdpb,speby->sqedy", second_table, shaped, precision=highest)
    spectrum = joined.reshape(signals * 2, 2, tok_rows, channels)
    return spectrum.reshape(spectrum.shape[0] // 2, 2, 2, tok_rows, series.shape[-1])


def inverse_series(spectra):
    devices = lax.axis_size("ctx")
    signals = spectra.shape[0]
    tok_rows = spectra.shape[3]
    channels_all = spectra.shape[4]
    group_rows = tok_rows // devices
    classes = 2 * devices
    fft_length = classes * tok_rows
    ordering = class_order(devices)
    norm_factor = 1.0 / math.sqrt(fft_length)
    location = lax.axis_index("ctx")
    own_classes = jnp.stack(
        [
            jnp.where(location == 0, 0, location),
            jnp.where(location == 0, devices, classes - location),
        ]
    )
    rows_index = jnp.arange(tok_rows, dtype=jnp.int32)
    square_turns = rows_index[:, None] * rows_index[None, :] * classes % fft_length
    second_turns = (
        square_turns[None, :, :] + own_classes[:, None, None] * rows_index[None, :, None]
    ) % fft_length
    second_angle = second_turns.astype(jnp.float32) * (2.0 * math.pi / fft_length)
    cos_second = jnp.cos(second_angle)
    sin_second = jnp.sin(second_angle)
    second_table = jnp.stack(
        [jnp.stack([cos_second, -sin_second], axis=2), jnp.stack([sin_second, cos_second], axis=2)],
        axis=1,
    )
    stacked = jnp.einsum("eqbpd,spedy->sqeby", second_table, spectra, precision=highest)
    stacked = stacked.reshape(signals * 2, 1, 2, tok_rows, channels_all)
    first_angle = 2.0 * np.pi * (np.outer(np.arange(devices), ordering) % classes) / classes
    cos_first = np.cos(first_angle)
    sin_first = np.sin(first_angle)
    full_table = (
        np.stack(
            [np.stack([cos_first, -sin_first], axis=1), np.stack([sin_first, cos_first], axis=1)]
        )
        * norm_factor
    )
    first_table = jnp.asarray(full_table, jnp.float32)
    received = lax.all_to_all(stacked, "ctx", split_axis=3, concat_axis=1, tiled=True)
    channels = received.shape[-1]
    flattened = received.reshape(signals, 2, classes, group_rows * channels)
    time_series = jnp.einsum("qapj,spjx->sqax", first_table, flattened, precision=highest)
    time_series = time_series.reshape(2, devices, group_rows, channels)
    outputs = lax.all_to_all(time_series, "ctx", split_axis=1, concat_axis=1, tiled=True)
    return outputs.reshape(2, tok_rows, channels_all)


def narrow_shards(query_series, key_series, value_series, grad_out, gate_mask, filter_spectrum):
    gating = gate_mask.astype(jnp.float32)[:, None]
    gated_pair = (
        gating * key_series.astype(jnp.float32) * value_series.astype(jnp.float32)
    ).astype(jnp.bfloat16)
    back_signal = (query_series.astype(jnp.float32) * grad_out.astype(jnp.float32)).astype(
        jnp.bfloat16
    )
    series = jnp.stack([gated_pair, back_signal])
    filter_real = filter_spectrum[0]
    filter_imag = filter_spectrum[1]
    combined = forward_spectra(series)[0]
    mirror = partner(combined)
    signal_real = 0.5 * (combined[0] + mirror[0])
    signal_imag = 0.5 * (combined[1] - mirror[1])
    adjoint_real = 0.5 * (combined[1] + mirror[1])
    adjoint_imag = 0.5 * (mirror[0] - combined[0])
    conv_real = signal_real * filter_real - signal_imag * filter_imag
    conv_imag = signal_real * filter_imag + signal_imag * filter_real
    back_real = adjoint_real * filter_real + adjoint_imag * filter_imag
    back_imag = adjoint_imag * filter_real - adjoint_real * filter_imag
    grad_spectrum = jnp.stack(
        [
            adjoint_real * signal_real + adjoint_imag * signal_imag,
            adjoint_imag * signal_real - adjoint_real * signal_imag,
        ]
    )
    minus_pair = jnp.stack([conv_real + back_imag, conv_imag - back_real])
    mirror_back = partner(minus_pair)
    joined = jnp.stack(
        [
            0.5 * (conv_real - back_imag + mirror_back[0]),
            0.5 * (conv_imag + back_real - mirror_back[1]),
        ]
    )
    outputs = inverse_series(joined[None])
    conv_out = outputs[0]
    grad_mixed = outputs[1]
    mixer_out = (query_series.astype(jnp.float32) * conv_out).astype(jnp.bfloat16)
    grad_queries = (grad_out.astype(jnp.float32) * conv_out).astype(jnp.bfloat16)
    grad_keys = (grad_mixed * gating * value_series.astype(jnp.float32)).astype(jnp.bfloat16)
    grad_values = (grad_mixed * gating * key_series.astype(jnp.float32)).astype(jnp.bfloat16)
    return (mixer_out, grad_queries, grad_keys, grad_values, grad_spectrum)


SUB = 16
LANES = 128


def split_table(values):
    exact = np.asarray(values, np.float32)
    high = exact.astype(jnp.bfloat16)
    low = (exact - high.astype(np.float32)).astype(jnp.bfloat16)
    return np.stack([high, low], axis=-3)


def device_tables(devices):
    classes = 2 * devices
    turns = 2.0 * np.pi * (np.outer(np.arange(devices), np.arange(devices)) % classes) / classes
    small = np.stack([np.cos(turns), -np.sin(turns)], axis=1)
    small[0, 1] = np.where(np.arange(devices) % 2 == 0, 1.0, -1.0)
    small = small.reshape(classes, devices)
    full = np.kron(small, np.eye(SUB))
    return split_table(full), split_table(full.T)


def row_tables(devices, rows):
    classes = 2 * devices
    length = classes * rows
    half = rows // 2
    place = np.arange(rows)
    tables = np.zeros((devices, 2, rows, 2, rows))
    for group in range(1, devices):
        freq = group + classes * place
        angle = 2.0 * np.pi * (np.outer(freq, place) % length) / length
        tables[group, 0, :, 0] = np.cos(angle)
        tables[group, 0, :, 1] = np.sin(angle)
        tables[group, 1, :, 0] = -np.sin(angle)
        tables[group, 1, :, 1] = np.cos(angle)
    for part, first in ((0, 0), (1, devices)):
        freq = first + classes * np.arange(half)
        angle = 2.0 * np.pi * (np.outer(freq, place) % length) / length
        tables[0, 0, part * half : (part + 1) * half, part] = np.cos(angle)
        tables[0, 1, part * half : (part + 1) * half, part] = -np.sin(angle)
    tables[0, 1, 0, 0] = np.where(place % 2 == 0, 1.0, -1.0)
    tables = tables.reshape(devices, 2 * rows, 2 * rows) / math.sqrt(length)
    return split_table(tables), split_table(tables.transpose(0, 2, 1))


def fold_tables(rows):
    half = rows // 2
    fold = np.zeros((2, 2, rows, 2, 2, rows))
    spread = np.zeros((2, 2, 2, rows, 2, rows))
    for d in range(rows):
        for part, sign in ((0, 1.0), (1, -1.0)):
            fold[1, part, d, part, 0, d] = 1.0
            fold[1, part, d, part, 1, rows - 1 - d] = sign
            spread[1, part, 0, d, part, d] = 1.0
            spread[1, part, 1, rows - 1 - d, part, d] = sign
    for d in range(half):
        for part, sign in ((0, 1.0), (1, -1.0)):
            if d > 0:
                fold[0, part, d, part, 0, d] = 1.0
                fold[0, part, d, part, 0, rows - d] = sign
                spread[0, part, 0, d, part, d] = 1.0
                spread[0, part, 0, rows - d, part, d] = sign
            fold[0, part, half + d, part, 1, d] = 1.0
            fold[0, part, half + d, part, 1, rows - 1 - d] = sign
            spread[0, part, 1, d, part, half + d] = 1.0
            spread[0, part, 1, rows - 1 - d, part, half + d] = sign
    fold[0, 0, 0, 0, 0, 0] = 1.0
    fold[0, 1, 0, 0, 0, half] = 1.0
    spread[0, 0, 0, 0, 0, 0] = 1.0
    spread[0, 0, 0, half, 1, 0] = 1.0
    return (
        fold.reshape(2, 2 * rows, 4 * rows).astype(jnp.bfloat16),
        spread.reshape(2, 4 * rows, 2 * rows).astype(jnp.bfloat16),
    )


def dot(left, right):
    return jnp.dot(left, right, preferred_element_type=jnp.float32)


def gate_column(mask):
    rows = mask.shape[1]
    across = lax.broadcasted_iota(jnp.int32, (rows, rows), 1)
    down = lax.broadcasted_iota(jnp.int32, (rows, rows), 0)
    spots = jnp.where(across == down, mask.astype(jnp.float32), 0.0)
    return jnp.sum(spots, axis=1, keepdims=True)


def exchange_kernel(
    devices,
    groups,
    rows,
    width,
    gate_ref,
    query_hbm,
    key_hbm,
    value_hbm,
    grad_hbm,
    fold_hbm,
    filter_hbm,
    mix_hbm,
    table_hbm,
    back_hbm,
    unmix_hbm,
    got_grad,
    got_series,
    query_ref,
    key_ref,
    value_ref,
    grad_ref,
    fold_ref,
    filter_ref,
    mix_ref,
    table_ref,
    back_ref,
    unmix_ref,
    send_signal,
    got_signal,
    send_filter,
    got_filter,
    mixed,
    turned,
    send_grad,
    send_series,
    send_sems,
    recv_sems,
    local_sems,
):
    me = lax.axis_index("ctx")
    lane = lax.axis_index("grp")
    barrier = pltpu.get_barrier_semaphore()
    own_fold = jnp.where(me == 0, 0, 1)
    loads = [
        pltpu.make_async_copy(source, target, local_sems.at[2 + at])
        for at, (source, target) in enumerate(
            (
                (query_hbm, query_ref),
                (key_hbm, key_ref),
                (value_hbm, value_ref),
                (grad_hbm, grad_ref),
                (fold_hbm.at[own_fold], fold_ref),
                (filter_hbm, filter_ref),
                (mix_hbm, mix_ref),
                (table_hbm, table_ref),
                (back_hbm, back_ref),
                (unmix_hbm, unmix_ref),
            )
        )
    ]
    for load in loads:
        load.start()

    def greet(step, _):
        pl.semaphore_signal(
            barrier,
            inc=1,
            device_id={"ctx": lax.rem(me + step, devices)},
            device_id_type=pl.DeviceIdType.MESH,
        )
        return 0

    lax.fori_loop(1, devices, greet, 0)
    for step in range(1, groups):
        pl.semaphore_signal(
            barrier,
            inc=1,
            device_id={"grp": lax.rem(lane + step, groups)},
            device_id_type=pl.DeviceIdType.MESH,
        )

    near = devices // 2
    side = me // near
    spot = lax.rem(me, near)

    def partner_at(step, direction):
        step = step + step // near
        half_at = lax.rem(side + 1 + step // near, 2)
        return half_at * near + lax.rem(spot + near + direction * lax.rem(step, near), near)

    def remote(kind, source, target, step_from, to):
        return pltpu.make_async_remote_copy(
            src_ref=source.at[to],
            dst_ref=target.at[step_from],
            send_sem=send_sems.at[kind, to],
            recv_sem=recv_sems.at[kind, step_from],
            device_id={"ctx": to},
            device_id_type=pl.DeviceIdType.MESH,
        )

    def relay(step, group):
        return pltpu.make_async_remote_copy(
            src_ref=got_filter.at[group],
            dst_ref=got_filter.at[group],
            send_sem=send_sems.at[3 + step, group],
            recv_sem=recv_sems.at[1, group],
            device_id={"grp": lax.rem(lane + step, groups)},
            device_id_type=pl.DeviceIdType.MESH,
        )

    def start_all(kind, source, target):
        def body(step, _):
            remote(kind, source, target, me, partner_at(step, 1)).start()
            return 0

        lax.fori_loop(0, devices - 1, body, 0)

    def wait_received(kind, source, target):
        def body(step, _):
            other = partner_at(step, -1)
            remote(kind, source, target, other, other).wait_recv()
            return 0

        lax.fori_loop(0, devices - 1, body, 0)

    def wait_sent(kind, source, target):
        def body(step, _):
            remote(kind, source, target, me, partner_at(step, 1)).wait_send()
            return 0

        lax.fori_loop(0, devices - 1, body, 0)

    for load in loads[:4]:
        load.wait()
    gating = gate_column(gate_ref[...])

    def make_signal(to):
        span = pl.ds(pl.multiple_of(to * width, width), width)
        gated = gating * key_ref[:, span].astype(jnp.float32) * value_ref[:, span].astype(jnp.float32)
        back = query_ref[:, span].astype(jnp.float32) * grad_ref[:, span].astype(jnp.float32)
        return gated.astype(jnp.bfloat16), back.astype(jnp.bfloat16)

    pl.semaphore_wait(barrier, devices + groups - 2)

    def ship_signal(step, _):
        to = partner_at(step, 1)
        send_signal[to, 0], send_signal[to, 1] = make_signal(to)
        remote(0, send_signal, got_signal, me, to).start()
        return 0

    lax.fori_loop(0, devices - 1, ship_signal, 0)
    got_signal[me, 0], got_signal[me, 1] = make_signal(me)

    for load in loads[4:6]:
        load.wait()
    mine = lax.rem(me, groups) == lane

    @pl.when(mine)
    def _():
        for to in range(devices):
            span = slice(to * width, (to + 1) * width)
            block = filter_ref[:, span]
            high = block.astype(jnp.bfloat16)
            low = (block - high.astype(jnp.float32)).astype(jnp.bfloat16)
            folded = dot(fold_ref[...], high) + dot(fold_ref[...], low)
            send_filter[to] = folded.astype(jnp.bfloat16)
        start_all(1, send_filter, got_filter)
        got_filter[me] = send_filter[me]

    for load in loads[6:]:
        load.wait()
    wait_received(0, send_signal, got_signal)

    def mix(part, _):
        span = pl.ds(pl.multiple_of(part * SUB, SUB), SUB)
        columns = jnp.concatenate(
            [got_signal[:, which, span, :].reshape(devices * SUB, width) for which in (0, 1)], axis=1
        )
        result = dot(mix_ref[0], columns) + dot(mix_ref[1], columns)
        mixed[:, span, :] = result.astype(jnp.bfloat16).reshape(2 * devices, SUB, 2 * width)
        return 0

    lax.fori_loop(0, rows // SUB, mix, 0)

    row_index = lax.broadcasted_iota(jnp.int32, (rows, width), 0)

    def one_group(group):
        source = mixed[pl.ds(2 * group, 2)].reshape(2 * rows, 2 * width)
        spectra = dot(table_ref[group, 0], source) + dot(table_ref[group, 1], source)
        signal_real = spectra[:rows, :width]
        signal_imag = spectra[rows:, :width]
        adjoint_real = spectra[:rows, width:]
        adjoint_imag = spectra[rows:, width:]
        response = got_filter[group].astype(jnp.float32)
        filter_real = response[:rows]
        filter_imag = response[rows:]
        real_pair = jnp.logical_and(row_index == 0, group == 0)

        def times(first_real, first_imag, second_real, second_imag, sign):
            both = first_imag * second_imag
            real = first_real * second_real - jnp.where(real_pair, 0.0, sign * both)
            imag = jnp.where(real_pair, both, first_imag * second_real + sign * first_real * second_imag)
            return real, imag

        grad_real, grad_imag = times(adjoint_real, adjoint_imag, signal_real, signal_imag, -1.0)
        send_grad[group, :rows] = grad_real.astype(jnp.bfloat16)
        send_grad[group, rows:] = grad_imag.astype(jnp.bfloat16)

        @pl.when(group != me)
        def _():
            remote(2, send_grad, got_grad, me, group).start()

        conv_real, conv_imag = times(signal_real, signal_imag, filter_real, filter_imag, 1.0)
        back_real, back_imag = times(adjoint_real, adjoint_imag, filter_real, filter_imag, -1.0)
        product = jnp.concatenate(
            [
                jnp.concatenate([conv_real, back_real], axis=1),
                jnp.concatenate([conv_imag, back_imag], axis=1),
            ],
            axis=0,
        ).astype(jnp.bfloat16)
        result = dot(back_ref[group, 0], product) + dot(back_ref[group, 1], product)
        turned[pl.ds(2 * group, 2)] = result.astype(jnp.bfloat16).reshape(2, rows, 2 * width)

    turns = near // groups

    def in_turn(shift):
        share = lax.rem(lane + shift, groups)

        def body(turn, _):
            half_at = lax.rem(side + 1 + turn // turns, 2)
            place = lax.rem(spot // groups + turns - lax.rem(turn, turns), turns)
            group = half_at * near + place * groups + share

            if shift == 0:

                @pl.when(group != me)
                def _():
                    remote(1, send_filter, got_filter, group, group).wait_recv()

                for step in range(1, groups):
                    relay(step, group).start()
            else:
                relay(shift, group).wait_recv()
            one_group(group)
            return 0

        return body

    for shift in range(groups):
        lax.fori_loop(0, devices // groups, in_turn(shift), 0)
    own_grad = pltpu.make_async_copy(send_grad.at[me], got_grad.at[me], local_sems.at[0])
    own_grad.start()

    def unmix(part, _):
        span = pl.ds(pl.multiple_of(part * SUB, SUB), SUB)
        columns = turned[:, span, :].reshape(2 * devices * SUB, 2 * width)
        result = dot(unmix_ref[0], columns) + dot(unmix_ref[1], columns)
        result = result.astype(jnp.bfloat16).reshape(devices, SUB, 2 * width)
        send_series[:, 0, span, :] = result[:, :, :width]
        send_series[:, 1, span, :] = result[:, :, width:]
        return 0

    lax.fori_loop(0, rows // SUB, unmix, 0)
    start_all(3, send_series, got_series)
    own_series = pltpu.make_async_copy(send_series.at[me], got_series.at[me], local_sems.at[1])
    own_series.start()
    own_grad.wait()
    own_series.wait()
    wait_received(2, send_grad, got_grad)
    wait_received(3, send_series, got_series)
    wait_sent(0, send_signal, got_signal)

    @pl.when(mine)
    def _():
        wait_sent(1, send_filter, got_filter)

    def relays_sent(turn, _):
        for step in range(1, groups):
            relay(step, turn * groups + lane).wait_send()
        return 0

    lax.fori_loop(0, devices // groups, relays_sent, 0)
    wait_sent(2, send_grad, got_grad)
    wait_sent(3, send_series, got_series)


def finish_kernel(
    blocks,
    width,
    query_ref,
    key_ref,
    value_ref,
    grad_ref,
    gate_ref,
    spread_ref,
    half_ref,
    series_ref,
    mixer_out,
    queries_out,
    keys_out,
    values_out,
    spectrum_out,
):
    gating = gate_column(gate_ref[...])
    own_spread = jnp.where(lax.axis_index("ctx") == 0, 0, 1)
    for block in range(blocks):
        span = slice(block * width, (block + 1) * width)
        conv = series_ref[block, 0].astype(jnp.float32)
        back = series_ref[block, 1].astype(jnp.float32) * gating
        mixer_out[:, span] = (query_ref[:, span].astype(jnp.float32) * conv).astype(jnp.bfloat16)
        queries_out[:, span] = (grad_ref[:, span].astype(jnp.float32) * conv).astype(jnp.bfloat16)
        keys_out[:, span] = (back * value_ref[:, span].astype(jnp.float32)).astype(jnp.bfloat16)
        values_out[:, span] = (back * key_ref[:, span].astype(jnp.float32)).astype(jnp.bfloat16)

    for first in range(0, blocks, 2):
        halves = jnp.concatenate([half_ref[block] for block in range(first, min(first + 2, blocks))], axis=1)
        spectrum_out[:, first * width : first * width + halves.shape[1]] = dot(spread_ref[own_spread], halves)


def wide_shards(query_series, key_series, value_series, grad_out, gate_mask, filter_spectrum):
    devices = lax.axis_size("ctx")
    rows, channels = query_series.shape
    width = channels // devices
    gating = gate_mask[None, :]
    mix_table, unmix_table = device_tables(devices)
    forward_table, back_table = row_tables(devices, rows)
    folds, spreads = fold_tables(rows)
    groups = lax.axis_size("grp")
    half = jnp.bfloat16
    vmem = pl.BlockSpec(memory_space=pltpu.VMEM)
    anywhere = pl.BlockSpec(memory_space=pl.ANY)
    spectrum_block = (devices, 2 * rows, width)
    series_block = (devices, 2, rows, width)
    got_grad, got_series = pl.pallas_call(
        functools.partial(exchange_kernel, devices, groups, rows, width),
        out_shape=(
            jax.ShapeDtypeStruct(spectrum_block, half),
            jax.ShapeDtypeStruct(series_block, half),
        ),
        in_specs=[vmem] + [anywhere] * 10,
        out_specs=(anywhere, anywhere),
        scratch_shapes=[pltpu.VMEM((rows, channels), half)] * 4
        + [
            pltpu.VMEM((2 * rows, 4 * rows), half),
            pltpu.VMEM((4 * rows, channels), jnp.float32),
            pltpu.VMEM(mix_table.shape, half),
            pltpu.VMEM(forward_table.shape, half),
            pltpu.VMEM(back_table.shape, half),
            pltpu.VMEM(unmix_table.shape, half),
            pltpu.VMEM(series_block, half),
            pltpu.VMEM(series_block, half),
            pltpu.VMEM(spectrum_block, half),
            pltpu.VMEM(spectrum_block, half),
            pltpu.VMEM((2 * devices, rows, 2 * width), half),
            pltpu.VMEM((2 * devices, rows, 2 * width), half),
            pltpu.VMEM(spectrum_block, half),
            pltpu.VMEM(series_block, half),
            pltpu.SemaphoreType.DMA((3 + groups, devices)),
            pltpu.SemaphoreType.DMA((4, devices)),
            pltpu.SemaphoreType.DMA((12,)),
        ],
        compiler_params=pltpu.CompilerParams(
            collective_id=0, has_side_effects=True, vmem_limit_bytes=60 * 1024 * 1024
        ),
        name="exchange",
    )(
        gating,
        query_series,
        key_series,
        value_series,
        grad_out,
        jnp.asarray(folds),
        filter_spectrum.reshape(4 * rows, channels),
        jnp.asarray(mix_table),
        jnp.asarray(forward_table),
        jnp.asarray(back_table),
        jnp.asarray(unmix_table),
    )
    blocks = math.gcd(devices, 4)
    columns = pl.BlockSpec((rows, blocks * width), lambda step: (0, step))
    mixer_out, queries, keys, values, spectrum = pl.pallas_call(
        functools.partial(finish_kernel, blocks, width),
        grid=(devices // blocks,),
        out_shape=(jax.ShapeDtypeStruct((rows, channels), half),) * 4
        + (jax.ShapeDtypeStruct((4 * rows, channels), jnp.float32),),
        in_specs=[
            columns,
            columns,
            columns,
            columns,
            pl.BlockSpec((1, rows), lambda step: (0, 0)),
            pl.BlockSpec((2, 4 * rows, 2 * rows), lambda step: (0, 0, 0)),
            pl.BlockSpec((blocks, 2 * rows, width), lambda step: (step, 0, 0)),
            pl.BlockSpec((blocks, 2, rows, width), lambda step: (step, 0, 0, 0)),
        ],
        out_specs=(columns,) * 4 + (pl.BlockSpec((4 * rows, blocks * width), lambda step: (0, step)),),
        compiler_params=pltpu.CompilerParams(vmem_limit_bytes=60 * 1024 * 1024),
        name="finish",
    )(query_series, key_series, value_series, grad_out, gating, jnp.asarray(spreads), got_grad, got_series)
    return mixer_out, queries, keys, values, spectrum.reshape(2, 2, rows, channels)


def shards(query_series, *others):
    devices = lax.axis_size("ctx")
    rows, channels = query_series.shape
    if rows % SUB == 0 and channels % (devices * LANES) == 0 and devices % (2 * lax.axis_size("grp")) == 0:
        return wide_shards(query_series, *others)
    return narrow_shards(query_series, *others)


def solution(mesh):
    placed = (
        P(("grp", "ctx"), None),
        P(("grp", "ctx"), None),
        P(("grp", "ctx"), None),
        P(("grp", "ctx"), None),
        P(("grp", "ctx")),
        P(None, "ctx", None, None),
    )
    return jax.shard_map(
        shards,
        mesh=mesh,
        in_specs=placed,
        out_specs=(
            P(("grp", "ctx"), None),
            P(("grp", "ctx"), None),
            P(("grp", "ctx"), None),
            P(("grp", "ctx"), None),
            P(None, ("grp", "ctx"), None, None),
        ),
        check_vma=False,
    )
```
